512 devices in a mesh: rep: 64 (over z, y_hi, core), mp: 8 (over y_lo, x).
Axes of the slice: x: 4, y: 8 (y_hi: 4, y_lo: 2; y = y_hi * 2 + y_lo), z: 8, core: 2. Of those that a mesh axis runs over, the one named last changes fastest.
Arguments:
- momentum: float32 [64, 2, 128, 5120], P('rep', None, None, 'mp'), may hold values from -6 to 6
- gradient: bfloat16 [64, 2, 128, 5120], P('rep', None, None, 'mp')
- kept_index: int32 [64], replicated, may hold values from 0 to 4095, as said below
Outputs:
- new_momentum: float32 [64, 2, 128, 5120], P('rep', None, None, 'mp')
- update: bfloat16 [2, 128, 5120], P(None, None, 'mp')
The draws below stay inside these ranges and needn't reach their ends.
Inputs may be any that keep to these rules, and one draw needn't show every extreme that they name: `kept_index`: 64 distinct indices u * 64 + v, for row frequency u and column frequency v.
All inputs are finite; a program needn't handle non-finite values. Where the reference program divides by a largest or mean magnitude, that divisor is 1e-20 or more.
Results may differ from the reference program's by a relative error of at most 0.001.
Values sent between devices are 32-bit elements; how exact they have to be, the bound alone decides.
No kernel may reach another device: no remote copies, remote signals or barrier semaphores. Data moves between devices by JAX's collectives and lax.ppermute only.
A program may use at most 64 MiB of HBM per device.

```python
import math
import jax
import jax.numpy as jnp
from jax import lax

D = 5120
GROUP = 64
KEEP = 64
LAYERS = 2
ROWS = 128
REPLICAS = 64


def draw_gradient(key, part):
    key = jax.random.fold_in(key, 11)
    key_noise = jax.random.fold_in(key, 0)
    key_rows = jax.random.fold_in(key, 1)
    key_cols = jax.random.fold_in(key, 2)
    key_order = jax.random.fold_in(key, 4)
    key_pairs = jax.random.fold_in(key, 5)
    shape = (REPLICAS, LAYERS, ROWS, D)
    row_scale = jnp.exp(jax.random.uniform(key_rows, (REPLICAS, LAYERS, ROWS, 1)) * math.log(10.0))
    col_scale = jnp.exp(jax.random.uniform(key_cols, (REPLICAS, LAYERS, 1, D)) * math.log(10.0))
    col_scale = col_scale * (1.0 + 2.0 * jnp.arange(D, dtype=jnp.float32) / D)
    pair_count = REPLICAS * LAYERS
    order = jax.random.permutation(key_order, pair_count).astype(jnp.float32)
    jitter = jax.random.uniform(key_pairs, (pair_count,))
    pair_scale = jnp.exp(-8.0 * (order + jitter) / pair_count).reshape(REPLICAS, LAYERS, 1, 1)
    noise = jax.random.normal(key_noise, shape)
    return (noise * row_scale * col_scale * pair_scale).astype(jnp.bfloat16)


def draw_kept_index(key, part):
    key = jax.random.fold_in(key, 7)
    return jax.random.permutation(key, GROUP * GROUP)[:KEEP].astype(jnp.int32)


def block_scale(own_key, dims, pieces, low, high):
    def one(position, parts):
        heights = jax.random.uniform(jax.random.fold_in(jax.random.fold_in(own_key, 6), position), (parts,), jnp.float32, low / len(pieces), high / len(pieces))
        return jnp.repeat(jnp.exp(heights), dims[position] // parts).reshape((-1,) + (1,) * (len(dims) - position - 1))

    level = one(*pieces[0])
    for cut in pieces[1:]:
        level = level * one(*cut)
    return level


def bell_draw(key, shape, spread, limit, cuts=(), kind=jnp.bfloat16):
    entries = jax.random.normal(key, shape, jnp.float32) * spread
    if len(cuts) > 0:
        entries = block_scale(key, shape, cuts, -0.22, 0.18) * entries
    return jnp.clip(entries, min=-limit, max=limit).astype(kind)


def setup_inputs(seed: int = 0) -> dict:
    keys = jax.random.split(jax.random.key(seed), 4)
    return {
        "momentum": bell_draw(keys[0], (REPLICAS, LAYERS, ROWS, D), 1.0, 6.0, ((0, 64), (3, 8)), jnp.float32),
        "gradient": draw_gradient(jax.random.fold_in(keys[3], 71), 0),
        "kept_index": draw_kept_index(jax.random.fold_in(keys[3], 71), 0),
    }


decay_rate = 0.999
epsilon = 1e-06
precise = lax.Precision.HIGHEST

def dct_matrix(order):
    freq = jnp.arange(order)[:, None]
    place = jnp.arange(order)[None, :]
    cosines = jnp.cos(jnp.pi * (2 * place + 1) * freq / (2 * order))
    scales = jnp.where(freq == 0, math.sqrt(1.0 / order), math.sqrt(2.0 / order))
    return (cosines * scales).astype(jnp.float32)

def reference(momentum, gradient, kept_index):
    cosines = dct_matrix(GROUP)
    row_c = cosines[kept_index // GROUP]
    col_c = cosines[kept_index % GROUP]

    def decode(spectra):
        return jnp.einsum('lacj,jm,jn->lamcn', spectra, row_c, col_c, precision=precise)

    def encode(blocks):
        full = jnp.einsum('um,lamcn,vn->lacuv', cosines, blocks, cosines, precision=precise)
        flattened = full.reshape(full.shape[:3] + (GROUP * GROUP,))
        return jnp.take(flattened, kept_index, axis=-1)

    def per_replica(pair):
        moment_old, grad_part = pair
        grad_wide = grad_part.astype(jnp.float32)
        mean_square = lax.optimization_barrier(jnp.mean(grad_wide * grad_wide, axis=(1, 2)))
        clip = 1.0 / jnp.maximum(1.0, jnp.sqrt(mean_square + epsilon))
        moment = decay_rate * moment_old + clip[:, None, None] * grad_wide
        blocks = moment.reshape(LAYERS, ROWS // GROUP, GROUP, D // GROUP, GROUP)
        spectra = encode(blocks)
        own_part = decode(spectra)
        return ((blocks - own_part).reshape(LAYERS, ROWS, D), spectra)
    new_momentum, spectra = lax.map(per_replica, (momentum, gradient))
    totals = lax.optimization_barrier(jnp.sum(spectra, axis=0))
    decoded = decode(totals)
    magnitude = lax.optimization_barrier(jnp.mean(jnp.abs(decoded), axis=(2, 4), keepdims=True))
    update = jnp.tanh(decoded / (magnitude + epsilon)).reshape(LAYERS, ROWS, D)
    return (new_momentum, update.astype(jnp.bfloat16))
```

```python
import math

import jax
import jax.numpy as jnp
import ml_dtypes
import numpy as np
from jax import lax
from jax.experimental import pallas as pl
from jax.experimental.pallas import tpu as pltpu
from jax.sharding import Mesh, PartitionSpec as P

GROUP = 64
LANES = 128
decay_rate = 0.999
epsilon = 1e-06
f32 = jnp.float32
bf16 = jnp.bfloat16
PARAMS = pltpu.CompilerParams(vmem_limit_bytes=24 * 1024 * 1024)


def dct_parts():
    freq = np.arange(GROUP)[:, None]
    place = np.arange(GROUP)[None, :]
    cosines = np.cos(np.pi * (2 * place + 1) * freq / (2 * GROUP))
    scales = np.where(freq == 0, math.sqrt(1.0 / GROUP), math.sqrt(2.0 / GROUP))
    rest = (cosines * scales).astype(np.float32).T
    parts = []
    for _ in range(3):
        part = rest.astype(ml_dtypes.bfloat16)
        parts.append(part)
        rest = rest - part.astype(np.float32)
    return parts


def halves(x):
    high = x.astype(bf16)
    return high, (x - high.astype(f32)).astype(bf16)


def times(x, b_high, b_low, transposed):
    dims = (((1,), (1 if transposed else 0,)), ((), ()))
    x_high, x_low = halves(x)
    dot = lambda a, b: lax.dot_general(a, b, dims, preferred_element_type=f32)
    return dot(x_high, b_high) + (dot(x_high, b_low) + dot(x_low, b_high))


def first_kernel(grad_ref, kept_ref, row_ref, col_ref, squares_ref, pick_ref, high_ref, low_ref):
    layers = grad_ref.shape[1]
    blocks = grad_ref.shape[3] // LANES
    rows = []
    for layer in range(layers):
        total = None
        for b in range(blocks):
            g = grad_ref[0, layer, :, b * LANES : (b + 1) * LANES].astype(f32)
            part = jnp.sum((g * g).reshape(-1, 8, LANES), axis=0)
            total = part if total is None else total + part
        rows.append(total[0:4] + total[4:8])
    part = jnp.concatenate(rows, axis=0)
    squares_ref[...] = jnp.broadcast_to(part[None], squares_ref.shape)

    kept = kept_ref[...]
    place = lax.broadcasted_iota(jnp.int32, (GROUP, LANES), 0)
    lane = lax.broadcasted_iota(jnp.int32, (GROUP, LANES), 1)
    row_hot = jnp.where(place == (kept >> 6), 1.0, 0.0).astype(bf16)
    col_hot = jnp.where(place == (kept & 63), 1.0, 0.0).astype(bf16)
    pick = None
    for i in range(3):
        term = jnp.dot(row_ref[i], row_hot, preferred_element_type=f32)
        pick = term if pick is None else pick + term
    pick_ref[...] = pick
    for i, ref in enumerate((high_ref, low_ref)):
        part = jnp.dot(col_ref[i], col_hot, preferred_element_type=f32)
        ref[...] = jnp.concatenate(
            [jnp.where(lane < GROUP, part, 0.0), jnp.where(lane < GROUP, 0.0, part)], axis=0
        ).astype(bf16)


def clips(squares_ref, layers, count):
    total = jnp.sum(squares_ref[...], axis=0)
    each = 8 // layers
    out = []
    for layer in range(layers):
        square = jnp.sum(total[layer * each : (layer + 1) * each], keepdims=True)
        out.append(1.0 / jnp.maximum(1.0, jnp.sqrt(square / count + epsilon)))
    return out


def moment_block(mom_ref, grad_ref, clip, b):
    lanes = slice(b * LANES, (b + 1) * LANES)
    return jnp.concatenate(
        [
            decay_rate * mom_ref[0, layer, :, lanes] + clip[layer] * grad_ref[0, layer, :, lanes].astype(f32)
            for layer in range(len(clip))
        ],
        axis=0,
    )


def encode_kernel(count, mom_ref, grad_ref, squares_ref, pick_ref, high_ref, low_ref, out_ref):
    layers = grad_ref.shape[1]
    blocks = grad_ref.shape[3] // LANES
    clip = clips(squares_ref, layers, count)
    pick = pick_ref[...]
    spectra = []
    for b in range(blocks):
        x = moment_block(mom_ref, grad_ref, clip, b)
        t = times(x, high_ref[...], low_ref[...], False)
        spectra.append(jnp.sum(t.reshape(-1, GROUP, LANES) * pick[None], axis=1))
    spectra.append(jnp.zeros_like(spectra[0]))
    half = len(spectra) // 2
    for i in range(half):
        both = jnp.concatenate([spectra[i], spectra[half + i]], axis=0)
        out_ref[:, :, i * LANES : (i + 1) * LANES] = jnp.broadcast_to(both[None], (out_ref.shape[0], 8, LANES))


def decode_block(spectra, pick, b_high, b_low):
    wide = (spectra[:, None, :] * pick[None]).reshape(-1, LANES)
    return times(wide, b_high, b_low, True)


def last_kernel(count, mom_ref, grad_ref, squares_ref, own_ref, total_ref, pick_ref, high_ref, low_ref, new_ref, update_ref):
    layers, rows = grad_ref.shape[1:3]
    blocks = grad_ref.shape[3] // LANES
    half = (blocks + 1) // 2
    clip = clips(squares_ref, layers, count)
    pick = pick_ref[...]
    b_high, b_low = high_ref[...], low_ref[...]
    own = own_ref[0]
    total = jnp.sum(total_ref[...], axis=0)

    def block(packed, b):
        lanes = slice((b % half) * LANES, (b % half + 1) * LANES)
        return packed[4:8, lanes] if b >= half else packed[0:4, lanes]

    lane = lax.broadcasted_iota(jnp.int32, (4, LANES), 1)
    for b in range(blocks):
        lanes = slice(b * LANES, (b + 1) * LANES)
        x = moment_block(mom_ref, grad_ref, clip, b)
        new = x - decode_block(block(own, b), pick, b_high, b_low)
        for layer in range(layers):
            new_ref[0, layer, :, lanes] = new[layer * rows : (layer + 1) * rows]
        d = decode_block(block(total, b), pick, b_high, b_low)
        tiles = d.reshape(4, GROUP, LANES)
        size = jnp.sum(jnp.abs(tiles), axis=1)
        left = jnp.sum(jnp.where(lane < GROUP, size, 0.0), axis=1, keepdims=True)
        right = jnp.sum(jnp.where(lane < GROUP, 0.0, size), axis=1, keepdims=True)
        mean = jnp.where(lane < GROUP, left, right) / (GROUP * GROUP)
        scale = 1.0 / (mean + epsilon)
        update = jnp.tanh(tiles * scale[:, None, :]).astype(bf16).reshape(layers, rows, LANES)
        update_ref[:, :, lanes] = update


def exchange(x, axes):
    return lax.all_to_all(x, axes, 0, 0, tiled=True)


def solution(mesh):
    whole = Mesh(mesh.devices.reshape(8, 4, 2, 2, 4), ("z", "yh", "core", "yl", "x"))
    rep, mp = ("z", "yh", "core"), ("yl", "x")
    parts = dct_parts()
    three = np.stack(parts)
    two = np.stack(parts[:2])

    def per_device(momentum, gradient, kept_index):
        _, layers, rows, cols = momentum.shape
        count = float(rows * cols * 8)
        kept = jnp.concatenate([kept_index, kept_index]).reshape(1, LANES)
        sds = jax.ShapeDtypeStruct
        squares, pick, high, low = pl.pallas_call(
            first_kernel,
            out_shape=(
                sds((8, 8, LANES), f32),
                sds((GROUP, LANES), f32),
                sds((LANES, LANES), bf16),
                sds((LANES, LANES), bf16),
            ),
            compiler_params=PARAMS,
            name="squares_and_picks",
        )(gradient, kept, three, two)
        squares = exchange(squares, mp)
        own = pl.pallas_call(
            lambda *refs: encode_kernel(count, *refs),
            out_shape=sds((8, 8, 3 * LANES), f32),
            compiler_params=PARAMS,
            name="encode",
        )(momentum, gradient, squares, pick, high, low)
        got = exchange(own, "z")
        some = jnp.broadcast_to(jnp.sum(got, axis=0, keepdims=True), got.shape)
        total = exchange(some, ("yh", "core"))
        return pl.pallas_call(
            lambda *refs: last_kernel(count, *refs),
            out_shape=(sds(momentum.shape, f32), sds((layers, rows, cols), bf16)),
            compiler_params=PARAMS,
            name="decode",
        )(momentum, gradient, squares, own, total, pick, high, low)

    return jax.shard_map(
        per_device,
        mesh=whole,
        in_specs=(P(rep, None, None, mp), P(rep, None, None, mp), P()),
        out_specs=(P(rep, None, None, mp), P(None, None, mp)),
        check_vma=False,
    )
```

```python
import math

import jax
import jax.numpy as jnp
from jax import lax
from jax.experimental import pallas as pl
from jax.experimental.pallas import tpu as pltpu
from jax.sharding import Mesh, PartitionSpec as P

GROUP = 64
LANES = 128
decay_rate = 0.999
epsilon = 1e-06
f32 = jnp.float32
bf16 = jnp.bfloat16
SHIFT = 256.0


def kept_cosines(freq, place):
    turn = ((2 * place + 1) * freq) & 255
    turn = jnp.where(turn > 128, 256 - turn, turn)
    far = turn > 64
    angle = jnp.where(far, 128 - turn, turn).astype(f32) * (math.pi / 128)
    square = angle * angle
    series = jnp.full_like(square, 1 / math.factorial(12))
    for n in (10, 8, 6, 4, 2, 0):
        series = series * square + (1 if n % 4 == 0 else -1) / math.factorial(n)
    scale = jnp.where(freq == 0, math.sqrt(1.0 / GROUP), math.sqrt(2.0 / GROUP))
    return jnp.where(far, -series, series) * scale


def halves(x):
    high = x.astype(bf16)
    return high, (x - high.astype(f32)).astype(bf16)


def dot(a, b, transposed=False):
    dims = (((1,), (1 if transposed else 0,)), ((), ()))
    return lax.dot_general(a, b, dims, preferred_element_type=f32)


def times(x, b_high, b_low, transposed=False):
    x_high, x_low = halves(x)
    return dot(x_high, b_high, transposed) + (dot(x_high, b_low, transposed) + dot(x_low, b_high, transposed))


def block(ref, b):
    lanes = slice(b * LANES, (b + 1) * LANES)
    return jnp.concatenate([ref[0, layer, :, lanes] for layer in range(ref.shape[1])], axis=0)


def squares_kernel(grad_ref, squares_ref):
    layers = grad_ref.shape[1]
    totals = []
    for layer in range(layers):
        wide = grad_ref[0, layer].astype(f32)
        parts = jnp.sum((wide * wide).reshape(-1, 8, wide.shape[1]), axis=0)
        total = parts[:, 0:LANES]
        for b in range(1, wide.shape[1] // LANES):
            total = total + parts[:, b * LANES : (b + 1) * LANES]
        totals.append(total[0:4] + total[4:8])
    squares_ref[...] = jnp.broadcast_to(jnp.concatenate(totals, axis=0)[None], squares_ref.shape)


def code_kernel(mom_ref, grad_ref, kept_ref, coded_ref, pick_ref, high_ref, low_ref):
    kept = kept_ref[...]
    kept = jnp.concatenate([kept, kept], axis=1)
    place = lax.broadcasted_iota(jnp.int32, (GROUP, LANES), 0)
    lane = lax.broadcasted_iota(jnp.int32, (GROUP, LANES), 1)
    pick = kept_cosines(kept >> 6, place)
    cols = kept_cosines(kept & 63, place) * (1 / SHIFT)
    both = jnp.concatenate([jnp.where(lane < GROUP, cols, 0.0), jnp.where(lane < GROUP, 0.0, cols)], axis=0)
    high, low = halves(both)
    pick_ref[...] = pick * (SHIFT * SHIFT)
    high_ref[...] = high
    low_ref[...] = low

    def gathered(t):
        return jnp.sum(t.reshape(-1, GROUP, LANES) * pick[None], axis=1)

    for b in range(grad_ref.shape[3] // LANES):
        lanes = slice(b * LANES, (b + 1) * LANES)
        g = block(grad_ref, b)
        coded_ref[4:8, lanes] = gathered(dot(g, high) + dot(g, low))
        coded_ref[0:4, lanes] = gathered(times(block(mom_ref, b), high, low))


def spectra_kernel(count, squares_ref, coded_ref, own_ref, clip_ref, pair_ref):
    clips = []
    members = squares_ref.shape[0] // 2
    for core in range(2):
        total = jnp.sum(squares_ref[core * members : (core + 1) * members], axis=0)
        squares = [jnp.sum(total[i : i + 4], keepdims=True) for i in (0, 4)]
        square = jnp.concatenate([jnp.broadcast_to(s, (4, LANES)) for s in squares], axis=0)
        clips.append(1.0 / jnp.maximum(1.0, jnp.sqrt(square / count + epsilon)))
        clip_ref[core] = clips[core]
    for b in range(coded_ref.shape[2] // LANES):
        lanes = slice(b * LANES, (b + 1) * LANES)
        both = []
        for core in range(2):
            both.append(decay_rate * coded_ref[core, 0:4, lanes] + clips[core][2:6] * coded_ref[core, 4:8, lanes])
            own_ref[core, :, lanes] = both[core]
        pair_ref[:, lanes] = both[0] + both[1]


def decode_block(spectra, pick, b_high, b_low):
    wide = (spectra[:, None, :] * pick[None]).reshape(-1, LANES)
    return times(wide, b_high, b_low, True)


def momentum_kernel(mom_ref, grad_ref, clip_ref, own_ref, pick_ref, high_ref, low_ref, new_ref):
    layers, rows = grad_ref.shape[1:3]
    for b in range(grad_ref.shape[3] // LANES):
        lanes = slice(b * LANES, (b + 1) * LANES)
        own = decode_block(own_ref[:, lanes], pick_ref[...], high_ref[...], low_ref[...])
        for layer in range(layers):
            each = clip_ref[4 * layer : 4 * layer + 1, :]
            x = decay_rate * mom_ref[0, layer, :, lanes] + each * grad_ref[0, layer, :, lanes].astype(f32)
            new_ref[0, layer, :, lanes] = x - own[layer * rows : (layer + 1) * rows]


def update_kernel(total_ref, pick_ref, high_ref, low_ref, update_ref):
    layers, rows, cols = update_ref.shape
    lane = lax.broadcasted_iota(jnp.int32, (4, LANES), 1)
    for b in range(cols // LANES):
        lanes = slice(b * LANES, (b + 1) * LANES)
        tiles = decode_block(total_ref[:, lanes], pick_ref[...], high_ref[...], low_ref[...]).reshape(4, GROUP, LANES)
        size = jnp.sum(jnp.abs(tiles), axis=1)
        left = jnp.sum(jnp.where(lane < GROUP, size, 0.0), axis=1, keepdims=True)
        right = jnp.sum(jnp.where(lane < GROUP, 0.0, size), axis=1, keepdims=True)
        mean = jnp.where(lane < GROUP, left, right) / (GROUP * GROUP)
        scale = 1.0 / (mean + epsilon)
        update_ref[:, :, lanes] = jnp.tanh(tiles * scale[:, None, :]).astype(bf16).reshape(layers, rows, LANES)


def exchange(x, axes):
    return lax.all_to_all(x, axes, 0, 0, tiled=True)


def solution(mesh):
    whole = Mesh(mesh.devices.reshape(8, 4, 2, 2, 4), ("z", "yh", "core", "yl", "x"))
    rep, mp = ("z", "yh", "core"), ("yl", "x")

    def per_device(momentum, gradient, kept_index):
        _, layers, rows, cols = momentum.shape
        count = float(rows * cols * 8)
        sds = jax.ShapeDtypeStruct

        def call(kernel, name, cost, *outs):
            return pl.pallas_call(
                kernel,
                out_shape=outs if len(outs) > 1 else outs[0],
                compiler_params=pltpu.CompilerParams(vmem_limit_bytes=24 * 1024 * 1024),
                cost_estimate=pl.CostEstimate(flops=cost, bytes_accessed=2 * momentum.size * 4, transcendentals=0),
                name=name,
            )

        squares = call(squares_kernel, "squares", 1 << 20, sds((16, 8, LANES), f32))(gradient)
        squares = exchange(squares, ("core",) + mp)
        coded, pick, high, low = call(
            code_kernel, "transforms", 1 << 28,
            sds((8, cols), f32), sds((GROUP, LANES), f32), sds((LANES, LANES), bf16), sds((LANES, LANES), bf16),
        )(momentum, gradient, kept_index.reshape(1, GROUP))
        coded = lax.all_gather(coded, "core")
        own, clip, pair = call(
            lambda *refs: spectra_kernel(count, *refs), "spectra", 1 << 20,
            sds((2, 4, cols), f32), sds((2, 8, LANES), f32), sds((4, cols), f32),
        )(squares, coded)
        core = lax.axis_index("core")
        part = lax.dynamic_slice_in_dim(pair, 2 * core, 2)
        got = exchange(jnp.broadcast_to(part[None], (32, 2, cols)), ("z", "yh"))
        own = lax.dynamic_index_in_dim(own, core, keepdims=False)
        clip = lax.dynamic_index_in_dim(clip, core, keepdims=False)
        new = call(momentum_kernel, "new_momentum", 1 << 28, sds(momentum.shape, f32))(
            momentum, gradient, clip, own, pick, high, low
        )
        total = lax.all_gather(jnp.sum(got, axis=0), "core", tiled=True)
        update = call(update_kernel, "update", 1 << 28, sds((layers, rows, cols), bf16))(total, pick, high, low)
        return new, update

    return jax.shard_map(
        per_device,
        mesh=whole,
        in_specs=(P(rep, None, None, mp), P(rep, None, None, mp), P()),
        out_specs=(P(rep, None, None, mp), P(None, None, mp)),
        check_vma=False,
    )
```

```python
import math

import jax
import jax.numpy as jnp
from jax import lax
from jax.experimental import pallas as pl
from jax.experimental.pallas import tpu as pltpu
from jax.sharding import Mesh, PartitionSpec as P

GROUP = 64
LANES = 128
decay_rate = 0.999
epsilon = 1e-06
f32 = jnp.float32
bf16 = jnp.bfloat16
SHIFT = 256.0


def kept_cosines(freq, place):
    turn = ((2 * place + 1) * freq) & 255
    turn = jnp.where(turn > 128, 256 - turn, turn)
    far = turn > 64
    angle = jnp.where(far, 128 - turn, turn).astype(f32) * (math.pi / 128)
    square = angle * angle
    series = jnp.full_like(square, 1 / math.factorial(12))
    for n in (10, 8, 6, 4, 2, 0):
        series = series * square + (1 if n % 4 == 0 else -1) / math.factorial(n)
    scale = jnp.where(freq == 0, math.sqrt(1.0 / GROUP), math.sqrt(2.0 / GROUP))
    return jnp.where(far, -series, series) * scale


def halves(x):
    high = x.astype(bf16)
    return high, (x - high.astype(f32)).astype(bf16)


def dot(a, b, transposed=False):
    dims = (((1,), (1 if transposed else 0,)), ((), ()))
    return lax.dot_general(a, b, dims, preferred_element_type=f32)


def times(x, wide, transposed=False):
    both = dot(jnp.concatenate(halves(x), axis=1), wide, transposed)
    return both[:, 0:LANES] + both[:, LANES : 2 * LANES]


def joined(high, low, transposed=False):
    zero = jnp.zeros_like(low)
    across, down = ((high, high), (low, zero)) if transposed else ((high, low), (high, zero))
    return jnp.concatenate([jnp.concatenate(across, axis=1), jnp.concatenate(down, axis=1)], axis=0)


def block(ref, b):
    lanes = slice(b * LANES, (b + 1) * LANES)
    return jnp.concatenate([ref[0, layer, :, lanes] for layer in range(ref.shape[1])], axis=0)


def first_kernel(mom_hbm, grad_hbm, kept_hbm, squares_hbm, mom_ref, grad_ref, pick_ref, code_ref, decode_ref, squares_ref, kept_ref, sems):
    layers = grad_ref.shape[1]
    copies = [pltpu.make_async_copy(grad_hbm.at[:, i], grad_ref.at[:, i], sems.at[i]) for i in range(layers)]
    copies += [pltpu.make_async_copy(kept_hbm, kept_ref, sems.at[layers])]
    copies += [pltpu.make_async_copy(mom_hbm, mom_ref, sems.at[layers + 1])]
    for copy in copies:
        copy.start()

    copies[layers].wait()
    kept = kept_ref[...]
    kept = jnp.concatenate([kept, kept], axis=1)
    place = lax.broadcasted_iota(jnp.int32, (GROUP, LANES), 0)
    lane = lax.broadcasted_iota(jnp.int32, (GROUP, LANES), 1)
    pick_ref[...] = kept_cosines(kept >> 6, place) * (SHIFT * SHIFT)
    cols = kept_cosines(kept & 63, place) * (1 / SHIFT)
    both = jnp.concatenate([jnp.where(lane < GROUP, cols, 0.0), jnp.where(lane < GROUP, 0.0, cols)], axis=0)
    high, low = halves(both)
    code_ref[...] = joined(high, low)
    decode_ref[...] = joined(high, low, transposed=True)

    for layer in range(layers):
        copies[layer].wait()
        wide = grad_ref[0, layer].astype(f32)
        parts = jnp.sum((wide * wide).reshape(-1, 8, wide.shape[1]), axis=0)
        total = parts[:, 0:LANES]
        for b in range(1, wide.shape[1] // LANES):
            total = total + parts[:, b * LANES : (b + 1) * LANES]
        total = total[0:4] + total[4:8]
        squares_ref[:, 4 * layer : 4 * layer + 4] = jnp.broadcast_to(total[None], (squares_ref.shape[0], 4, LANES))
    out = pltpu.make_async_copy(squares_ref, squares_hbm, sems.at[layers + 2])
    out.start()
    copies[-1].wait()
    out.wait()


def code_kernel(mom_ref, grad_ref, pick_ref, code_ref, coded_ref):
    pick = pick_ref[...] * (1 / (SHIFT * SHIFT))
    code = code_ref[...]

    def gathered(t):
        return jnp.sum(t.reshape(-1, GROUP, LANES) * pick[None], axis=1)

    for b in range(grad_ref.shape[3] // LANES):
        lanes = slice(b * LANES, (b + 1) * LANES)
        g = dot(block(grad_ref, b), code[0:LANES])
        coded_ref[4:8, lanes] = gathered(g[:, 0:LANES] + g[:, LANES : 2 * LANES])
        coded_ref[0:4, lanes] = gathered(times(block(mom_ref, b), code))


def spectra_kernel(count, squares_ref, coded_ref, copies_hbm, own_ref, clip_ref, copies_ref, sems):
    here = lax.axis_index("core")
    clips = []
    members = squares_ref.shape[0] // 2
    for core in range(2):
        total = jnp.sum(squares_ref[core * members : (core + 1) * members], axis=0)
        squares = [jnp.sum(total[i : i + 4], keepdims=True) for i in (0, 4)]
        square = jnp.concatenate([jnp.broadcast_to(s, (4, LANES)) for s in squares], axis=0)
        clips.append(1.0 / jnp.maximum(1.0, jnp.sqrt(square / count + epsilon)))
    clip_ref[...] = jnp.where(here == 0, clips[0], clips[1])
    for b in range(coded_ref.shape[2] // LANES):
        lanes = slice(b * LANES, (b + 1) * LANES)
        both = [decay_rate * coded_ref[core, 0:4, lanes] + clips[core][2:6] * coded_ref[core, 4:8, lanes] for core in range(2)]
        own_ref[:, lanes] = jnp.where(here == 0, both[0], both[1])
        pair = both[0] + both[1]
        part = jnp.where(here == 0, pair[0:2], pair[2:4])
        copies_ref[:, :, lanes] = jnp.broadcast_to(part[None], (copies_ref.shape[0], 2, LANES))
    size = copies_ref.shape[0]
    out = [pltpu.make_async_copy(copies_ref, copies_hbm.at[pl.ds(i * size, size)], sems.at[i]) for i in range(copies_hbm.shape[0] // size)]
    for copy in out:
        copy.start()
    for copy in out:
        copy.wait()


def decode_block(spectra, pick, decode):
    return times((spectra[:, None, :] * pick[None]).reshape(-1, LANES), decode, transposed=True)


def momentum_kernel(mom_ref, grad_ref, clip_ref, own_ref, pick_ref, decode_ref, new_ref):
    layers, rows = grad_ref.shape[1:3]
    for b in range(grad_ref.shape[3] // LANES):
        lanes = slice(b * LANES, (b + 1) * LANES)
        own = decode_block(own_ref[:, lanes], pick_ref[...], decode_ref[...])
        for layer in range(layers):
            each = clip_ref[4 * layer : 4 * layer + 1, :]
            x = decay_rate * mom_ref[0, layer, :, lanes] + each * grad_ref[0, layer, :, lanes].astype(f32)
            new_ref[0, layer, :, lanes] = x - own[layer * rows : (layer + 1) * rows]


def update_kernel(total_ref, pick_ref, decode_ref, update_hbm, update_ref, sems):
    layers, rows, cols = update_ref.shape
    lane = lax.broadcasted_iota(jnp.int32, (4, LANES), 1)
    copies = []
    for b in range(cols // LANES):
        lanes = slice(b * LANES, (b + 1) * LANES)
        tiles = decode_block(total_ref[:, lanes], pick_ref[...], decode_ref[...]).reshape(4, GROUP, LANES)
        size = jnp.sum(jnp.abs(tiles), axis=1)
        left = jnp.sum(jnp.where(lane < GROUP, size, 0.0), axis=1, keepdims=True)
        right = jnp.sum(jnp.where(lane < GROUP, 0.0, size), axis=1, keepdims=True)
        mean = jnp.where(lane < GROUP, left, right) / (GROUP * GROUP)
        scale = 1.0 / (mean + epsilon)
        update_ref[:, :, lanes] = jnp.tanh(tiles * scale[:, None, :]).astype(bf16).reshape(layers, rows, LANES)
        part = pl.ds(b * LANES, LANES)
        copies.append(pltpu.make_async_copy(update_ref.at[:, :, part], update_hbm.at[:, :, part], sems.at[b]))
        copies[b].start()
    for copy in copies:
        copy.wait()


def exchange(x, axes):
    return lax.all_to_all(x, axes, 0, 0, tiled=True)


def solution(mesh):
    whole = Mesh(mesh.devices.reshape(8, 4, 2, 2, 4), ("z", "yh", "core", "yl", "x"))
    rep, mp = ("z", "yh", "core"), ("yl", "x")

    def per_device(momentum, gradient, kept_index):
        _, layers, rows, cols = momentum.shape
        count = float(rows * cols * 8)
        sds = jax.ShapeDtypeStruct

        def call(kernel, name, cost, *outs):
            return pl.pallas_call(
                kernel,
                out_shape=outs if len(outs) > 1 else outs[0],
                compiler_params=pltpu.CompilerParams(vmem_limit_bytes=24 * 1024 * 1024),
                cost_estimate=pl.CostEstimate(flops=cost, bytes_accessed=2 * momentum.size * 4, transcendentals=0),
                name=name,
            )

        shapes = (momentum.shape, f32), (gradient.shape, bf16), ((GROUP, LANES), f32), ((2 * LANES, 2 * LANES), bf16), ((2 * LANES, 2 * LANES), bf16)
        hbm = lambda x: pltpu.with_memory_space_constraint(x, pltpu.HBM)
        squares, momentum, gradient, pick, code, decode = pl.pallas_call(
            first_kernel,
            in_specs=[pl.BlockSpec(memory_space=pltpu.HBM)] * 3,
            out_shape=(pltpu.HBM((16, 8, LANES), f32), *[pltpu.VMEM(*s) for s in shapes]),
            out_specs=(pl.BlockSpec(memory_space=pltpu.HBM),) + (pl.BlockSpec(memory_space=pltpu.VMEM),) * 5,
            scratch_shapes=[
                pltpu.VMEM((16, 8, LANES), f32),
                pltpu.VMEM((1, GROUP), jnp.int32),
                pltpu.SemaphoreType.DMA((layers + 3,)),
            ],
            compiler_params=pltpu.CompilerParams(vmem_limit_bytes=24 * 1024 * 1024),
            name="squares",
        )(hbm(momentum), hbm(gradient), hbm(kept_index.reshape(1, GROUP)))
        squares = exchange(squares, ("core",) + mp)
        coded = call(code_kernel, "transforms", 1 << 28, sds((8, cols), f32))(momentum, gradient, pick, code)
        coded = lax.all_gather(coded, "core")
        copies, own, clip = pl.pallas_call(
            lambda *refs: spectra_kernel(count, *refs),
            out_shape=(pltpu.HBM((32, 2, cols), f32), pltpu.VMEM((4, cols), f32), pltpu.VMEM((8, LANES), f32)),
            out_specs=(pl.BlockSpec(memory_space=pltpu.HBM),) + (pl.BlockSpec(memory_space=pltpu.VMEM),) * 2,
            scratch_shapes=[pltpu.VMEM((8, 2, cols), f32), pltpu.SemaphoreType.DMA((4,))],
            compiler_params=pltpu.CompilerParams(vmem_limit_bytes=24 * 1024 * 1024),
            name="spectra",
        )(squares, coded)
        got = exchange(copies, ("z", "yh"))
        new = call(momentum_kernel, "new_momentum", 1 << 28, sds(momentum.shape, f32))(
            momentum, gradient, clip, own, pick, decode
        )
        total = lax.all_gather(jnp.sum(got, axis=0), "core", tiled=True)
        update = pl.pallas_call(
            update_kernel,
            out_shape=pltpu.HBM((layers, rows, cols), bf16),
            out_specs=pl.BlockSpec(memory_space=pltpu.HBM),
            scratch_shapes=[pltpu.VMEM((layers, rows, cols), bf16), pltpu.SemaphoreType.DMA((cols // LANES,))],
            compiler_params=pltpu.CompilerParams(vmem_limit_bytes=24 * 1024 * 1024),
            name="update",
        )(total, pick, decode)
        return new, update

    return jax.shard_map(
        per_device,
        mesh=whole,
        in_specs=(P(rep, None, None, mp), P(rep, None, None, mp), P()),
        out_specs=(P(rep, None, None, mp), P(None, None, mp)),
        check_vma=False,
    )
```

```python
import math

import jax
import jax.numpy as jnp
from jax import lax
from jax.experimental import pallas as pl
from jax.experimental.pallas import tpu as pltpu
from jax.sharding import Mesh, PartitionSpec as P

GROUP = 64
LANES = 128
decay_rate = 0.999
epsilon = 1e-06
f32 = jnp.float32
bf16 = jnp.bfloat16
SHIFT = 256.0


def kept_cosines(freq, place):
    turn = ((2 * place + 1) * freq) & 255
    turn = jnp.where(turn > 128, 256 - turn, turn)
    far = turn > 64
    angle = jnp.where(far, 128 - turn, turn).astype(f32) * (math.pi / 128)
    square = angle * angle
    series = jnp.full_like(square, 1 / math.factorial(12))
    for n in (10, 8, 6, 4, 2, 0):
        series = series * square + (1 if n % 4 == 0 else -1) / math.factorial(n)
    scale = jnp.where(freq == 0, math.sqrt(1.0 / GROUP), math.sqrt(2.0 / GROUP))
    return jnp.where(far, -series, series) * scale


def halves(x):
    high = x.astype(bf16)
    return high, (x - high.astype(f32)).astype(bf16)


def dot(a, b, transposed=False):
    dims = (((1,), (1 if transposed else 0,)), ((), ()))
    return lax.dot_general(a, b, dims, preferred_element_type=f32)


def times(x, wide, transposed=False):
    both = dot(jnp.concatenate(halves(x), axis=1), wide, transposed)
    return both[:, 0:LANES] + both[:, LANES : 2 * LANES]


def joined(high, low, transposed=False):
    zero = jnp.zeros_like(low)
    across, down = ((high, high), (low, zero)) if transposed else ((high, low), (high, zero))
    return jnp.concatenate([jnp.concatenate(across, axis=1), jnp.concatenate(down, axis=1)], axis=0)


def block(ref, b):
    lanes = slice(b * LANES, (b + 1) * LANES)
    return jnp.concatenate([ref[0, layer, :, lanes] for layer in range(ref.shape[1])], axis=0)


def first_kernel(mom_hbm, grad_hbm, kept_hbm, squares_hbm, mom_ref, grad_ref, pick_ref, code_ref, decode_ref, squares_ref, kept_ref, sems):
    layers = grad_ref.shape[1]
    copies = [pltpu.make_async_copy(grad_hbm.at[:, i], grad_ref.at[:, i], sems.at[i]) for i in range(layers)]
    copies += [pltpu.make_async_copy(kept_hbm, kept_ref, sems.at[layers])]
    copies += [pltpu.make_async_copy(mom_hbm, mom_ref, sems.at[layers + 1])]
    for copy in copies:
        copy.start()

    copies[layers].wait()
    kept = kept_ref[...]
    kept = jnp.concatenate([kept, kept], axis=1)
    place = lax.broadcasted_iota(jnp.int32, (GROUP, LANES), 0)
    lane = lax.broadcasted_iota(jnp.int32, (GROUP, LANES), 1)
    pick_ref[...] = kept_cosines(kept >> 6, place) * (SHIFT * SHIFT)
    cols = kept_cosines(kept & 63, place) * (1 / SHIFT)
    both = jnp.concatenate([jnp.where(lane < GROUP, cols, 0.0), jnp.where(lane < GROUP, 0.0, cols)], axis=0)
    high, low = halves(both)
    code_ref[...] = joined(high, low)
    decode_ref[...] = joined(high, low, transposed=True)

    for layer in range(layers):
        copies[layer].wait()
        wide = grad_ref[0, layer].astype(f32)
        parts = jnp.sum((wide * wide).reshape(-1, 8, wide.shape[1]), axis=0)
        total = parts[:, 0:LANES]
        for b in range(1, wide.shape[1] // LANES):
            total = total + parts[:, b * LANES : (b + 1) * LANES]
        total = total[0:4] + total[4:8]
        squares_ref[:, 4 * layer : 4 * layer + 4] = jnp.broadcast_to(total[None], (squares_ref.shape[0], 4, LANES))
    out = pltpu.make_async_copy(squares_ref, squares_hbm, sems.at[layers + 2])
    out.start()
    copies[-1].wait()
    out.wait()


def code_kernel(mom_ref, grad_ref, pick_ref, code_ref, decode_ref, coded_ref, rest_mom_ref, rest_grad_ref):
    layers, rows = grad_ref.shape[1:3]
    wide_pick = pick_ref[...]
    pick = wide_pick * (1 / (SHIFT * SHIFT))
    code, decode = code_ref[...], decode_ref[...]

    def gathered(t):
        return jnp.sum(t.reshape(-1, GROUP, LANES) * pick[None], axis=1)

    for b in range(grad_ref.shape[3] // LANES):
        lanes = slice(b * LANES, (b + 1) * LANES)
        g = block(grad_ref, b)
        t = dot(g, code[0:LANES])
        coded_grad = gathered(t[:, 0:LANES] + t[:, LANES : 2 * LANES])
        m = block(mom_ref, b)
        coded_mom = gathered(times(m, code))
        coded_ref[4:8, lanes] = coded_grad
        coded_ref[0:4, lanes] = coded_mom
        rest_mom = decay_rate * (m - decode_block(coded_mom, wide_pick, decode))
        rest_grad = g.astype(f32) * (1 / SHIFT) - decode_block(coded_grad, pick, decode) * SHIFT
        for layer in range(layers):
            rest_mom_ref[0, layer, :, lanes] = rest_mom[layer * rows : (layer + 1) * rows]
            rest_grad_ref[0, layer, :, lanes] = rest_grad[layer * rows : (layer + 1) * rows]


def spectra_kernel(count, squares_ref, coded_ref, copies_ref, clip_ref):
    here = lax.axis_index("core")
    clips = []
    members = squares_ref.shape[0] // 2
    for core in range(2):
        total = jnp.sum(squares_ref[core * members : (core + 1) * members], axis=0)
        squares = [jnp.sum(total[i : i + 4], keepdims=True) for i in (0, 4)]
        square = jnp.concatenate([jnp.broadcast_to(s, (4, LANES)) for s in squares], axis=0)
        clips.append(1.0 / jnp.maximum(1.0, jnp.sqrt(square / count + epsilon)))
    clip_ref[...] = jnp.where(here == 0, clips[0], clips[1])
    for b in range(coded_ref.shape[2] // LANES):
        lanes = slice(b * LANES, (b + 1) * LANES)
        both = [decay_rate * coded_ref[core, 0:4, lanes] + clips[core][2:6] * coded_ref[core, 4:8, lanes] for core in range(2)]
        pair = both[0] + both[1]
        part = jnp.where(here == 0, pair[0:2], pair[2:4])
        copies_ref[:, :, lanes] = jnp.broadcast_to(part[None], (copies_ref.shape[0], 2, LANES))


def decode_block(spectra, pick, decode):
    return times((spectra[:, None, :] * pick[None]).reshape(-1, LANES), decode, transposed=True)


def last_kernel(rest_mom_ref, rest_grad_ref, clip_ref, total_ref, pick_ref, decode_ref, new_hbm, update_hbm, new_ref, update_ref, sems):
    layers, rows, cols = update_ref.shape
    copies = []
    for layer in range(layers):
        for b in range(cols // LANES):
            lanes = slice(b * LANES, (b + 1) * LANES)
            each = clip_ref[4 * layer : 4 * layer + 1, :]
            new_ref[0, layer, :, lanes] = rest_mom_ref[0, layer, :, lanes] + (each * rest_grad_ref[0, layer, :, lanes]) * SHIFT
        copies.append(pltpu.make_async_copy(new_ref.at[:, layer], new_hbm.at[:, layer], sems.at[layer]))
        copies[-1].start()
    lane = lax.broadcasted_iota(jnp.int32, (4, LANES), 1)
    for b in range(cols // LANES):
        lanes = slice(b * LANES, (b + 1) * LANES)
        tiles = decode_block(total_ref[:, lanes], pick_ref[...], decode_ref[...]).reshape(4, GROUP, LANES)
        size = jnp.sum(jnp.abs(tiles), axis=1)
        left = jnp.sum(jnp.where(lane < GROUP, size, 0.0), axis=1, keepdims=True)
        right = jnp.sum(jnp.where(lane < GROUP, 0.0, size), axis=1, keepdims=True)
        mean = jnp.where(lane < GROUP, left, right) / (GROUP * GROUP)
        scale = 1.0 / (mean + epsilon)
        update_ref[:, :, lanes] = jnp.tanh(tiles * scale[:, None, :]).astype(bf16).reshape(layers, rows, LANES)
        part = pl.ds(b * LANES, LANES)
        copies.append(pltpu.make_async_copy(update_ref.at[:, :, part], update_hbm.at[:, :, part], sems.at[layers + b]))
        copies[-1].start()
    for copy in copies:
        copy.wait()


def exchange(x, axes, groups):
    return lax.all_to_all(x, axes, 0, 0, axis_index_groups=groups, tiled=True)


def solution(mesh):
    whole = Mesh(mesh.devices.reshape(8, 4, 2, 2, 4), ("z", "yh", "core", "yl", "x"))
    rep, mp = ("z", "yh", "core"), ("yl", "x")

    first_groups = [[core * 8 + (yl ^ 1) * 4 + (x + 2) % 4 for core in range(2) for yl in range(2) for x in range(4)]]
    second_groups = [
        [(((z + 6) % 8) * 4 + (yh + 2) % 4) * 2 + core for z in range(8) for yh in range(4)] for core in range(2)
    ]

    def per_device(momentum, gradient, kept_index):
        _, layers, rows, cols = momentum.shape
        count = float(rows * cols * 8)
        sds = jax.ShapeDtypeStruct

        shapes = (momentum.shape, f32), (gradient.shape, bf16), ((GROUP, LANES), f32), ((2 * LANES, 2 * LANES), bf16), ((2 * LANES, 2 * LANES), bf16)
        hbm = lambda x: pltpu.with_memory_space_constraint(x, pltpu.HBM)
        squares, momentum, gradient, pick, code, decode = pl.pallas_call(
            first_kernel,
            in_specs=[pl.BlockSpec(memory_space=pltpu.HBM)] * 3,
            out_shape=(pltpu.HBM((16, 8, LANES), f32), *[pltpu.VMEM(*s) for s in shapes]),
            out_specs=(pl.BlockSpec(memory_space=pltpu.HBM),) + (pl.BlockSpec(memory_space=pltpu.VMEM),) * 5,
            scratch_shapes=[
                pltpu.VMEM((16, 8, LANES), f32),
                pltpu.VMEM((1, GROUP), jnp.int32),
                pltpu.SemaphoreType.DMA((layers + 3,)),
            ],
            compiler_params=pltpu.CompilerParams(vmem_limit_bytes=24 * 1024 * 1024),
            name="squares",
        )(hbm(momentum), hbm(gradient), hbm(kept_index.reshape(1, GROUP)))
        squares = exchange(squares, ("core",) + mp, first_groups)
        vmem = lambda *shapes: tuple(pltpu.VMEM(*s) for s in shapes)
        room = pltpu.CompilerParams(vmem_limit_bytes=24 * 1024 * 1024)
        coded, rest_mom, rest_grad = pl.pallas_call(
            code_kernel,
            out_shape=vmem(((8, cols), f32), (momentum.shape, f32), (momentum.shape, f32)),
            out_specs=(pl.BlockSpec(memory_space=pltpu.VMEM),) * 3,
            compiler_params=room,
            cost_estimate=pl.CostEstimate(flops=1 << 28, bytes_accessed=1 << 22, transcendentals=0),
            name="transforms",
        )(momentum, gradient, pick, code, decode)
        coded = lax.all_gather(coded, "core")
        copies, clip = pl.pallas_call(
            lambda *refs: spectra_kernel(count, *refs),
            out_shape=vmem(((32, 2, cols), f32), ((8, LANES), f32)),
            out_specs=(pl.BlockSpec(memory_space=pltpu.VMEM),) * 2,
            compiler_params=room,
            name="spectra",
        )(squares, coded)
        got = exchange(copies, rep, second_groups)
        total = lax.all_gather(jnp.sum(got, axis=0), "core", tiled=True)
        return pl.pallas_call(
            last_kernel,
            out_shape=(pltpu.HBM(momentum.shape, f32), pltpu.HBM((layers, rows, cols), bf16)),
            out_specs=(pl.BlockSpec(memory_space=pltpu.HBM),) * 2,
            scratch_shapes=[
                pltpu.VMEM(momentum.shape, f32),
                pltpu.VMEM((layers, rows, cols), bf16),
                pltpu.SemaphoreType.DMA((layers + cols // LANES,)),
            ],
            compiler_params=room,
            name="new_momentum_and_update",
        )(rest_mom, rest_grad, clip, total, pick, decode)

    return jax.shard_map(
        per_device,
        mesh=whole,
        in_specs=(P(rep, None, None, mp), P(rep, None, None, mp), P()),
        out_specs=(P(rep, None, None, mp), P(None, None, mp)),
        check_vma=False,
    )
```

```python
import math

import jax
import jax.numpy as jnp
from jax import lax
from jax.experimental import pallas as pl
from jax.experimental.pallas import tpu as pltpu
from jax.sharding import Mesh, PartitionSpec as P

GROUP = 64
LANES = 128
decay_rate = 0.999
epsilon = 1e-06
f32 = jnp.float32
bf16 = jnp.bfloat16
SHIFT = 256.0


def kept_cosines(freq, place):
    turn = ((2 * place + 1) * freq) & 255
    turn = jnp.where(turn > 128, 256 - turn, turn)
    far = turn > 64
    angle = jnp.where(far, 128 - turn, turn).astype(f32) * (math.pi / 128)
    square = angle * angle
    series = jnp.full_like(square, 1 / math.factorial(12))
    for n in (10, 8, 6, 4, 2, 0):
        series = series * square + (1 if n % 4 == 0 else -1) / math.factorial(n)
    scale = jnp.where(freq == 0, math.sqrt(1.0 / GROUP), math.sqrt(2.0 / GROUP))
    return jnp.where(far, -series, series) * scale


def halves(x):
    high = x.astype(bf16)
    return high, (x - high.astype(f32)).astype(bf16)


def dot(a, b, transposed=False):
    dims = (((1,), (1 if transposed else 0,)), ((), ()))
    return lax.dot_general(a, b, dims, preferred_element_type=f32)


def times(x, wide, transposed=False):
    both = dot(jnp.concatenate(halves(x), axis=1), wide, transposed)
    return both[:, 0:LANES] + both[:, LANES : 2 * LANES]


def joined(high, low, transposed=False):
    zero = jnp.zeros_like(low)
    across, down = ((high, high), (low, zero)) if transposed else ((high, low), (high, zero))
    return jnp.concatenate([jnp.concatenate(across, axis=1), jnp.concatenate(down, axis=1)], axis=0)


def block(ref, b):
    lanes = slice(b * LANES, (b + 1) * LANES)
    return jnp.concatenate([ref[0, layer, :, lanes] for layer in range(ref.shape[1])], axis=0)


def first_kernel(mom_hbm, grad_hbm, kept_hbm, squares_hbm, mom_ref, grad_ref, pick_ref, code_ref, decode_ref, squares_ref, kept_ref, sems):
    layers = grad_ref.shape[1]
    copies = [pltpu.make_async_copy(grad_hbm.at[:, i], grad_ref.at[:, i], sems.at[i]) for i in range(layers)]
    copies += [pltpu.make_async_copy(kept_hbm, kept_ref, sems.at[layers])]
    copies += [pltpu.make_async_copy(mom_hbm, mom_ref, sems.at[layers + 1])]
    for copy in copies:
        copy.start()

    copies[layers].wait()
    kept = kept_ref[...]
    kept = jnp.concatenate([kept, kept], axis=1)
    place = lax.broadcasted_iota(jnp.int32, (GROUP, LANES), 0)
    lane = lax.broadcasted_iota(jnp.int32, (GROUP, LANES), 1)
    pick_ref[...] = kept_cosines(kept >> 6, place) * (SHIFT * SHIFT)
    cols = kept_cosines(kept & 63, place) * (1 / SHIFT)
    both = jnp.concatenate([jnp.where(lane < GROUP, cols, 0.0), jnp.where(lane < GROUP, 0.0, cols)], axis=0)
    high, low = halves(both)
    code_ref[...] = joined(high, low)
    decode_ref[...] = joined(high, low, transposed=True)

    for layer in range(layers):
        copies[layer].wait()
        wide = grad_ref[0, layer].astype(f32)
        parts = jnp.sum((wide * wide).reshape(-1, 8, wide.shape[1]), axis=0)
        total = parts[:, 0:LANES]
        for b in range(1, wide.shape[1] // LANES):
            total = total + parts[:, b * LANES : (b + 1) * LANES]
        total = jnp.sum(total, axis=0, keepdims=True)
        squares_ref[:, layer : layer + 1] = jnp.broadcast_to(total[None], (squares_ref.shape[0], 1, LANES))
    out = pltpu.make_async_copy(squares_ref, squares_hbm, sems.at[layers + 2])
    out.start()
    copies[-1].wait()
    out.wait()


def code_kernel(mom_ref, grad_ref, pick_ref, code_ref, decode_ref, coded_ref, rest_mom_ref, rest_grad_ref):
    layers, rows = grad_ref.shape[1:3]
    wide_pick = pick_ref[...]
    pick = wide_pick * (1 / (SHIFT * SHIFT))
    code, decode = code_ref[...], decode_ref[...]

    def gathered(t):
        return jnp.sum(t.reshape(-1, GROUP, LANES) * pick[None], axis=1)

    for b in range(grad_ref.shape[3] // LANES):
        lanes = slice(b * LANES, (b + 1) * LANES)
        g = block(grad_ref, b)
        t = dot(g, code[0:LANES])
        coded_grad = gathered(t[:, 0:LANES] + t[:, LANES : 2 * LANES])
        m = block(mom_ref, b)
        coded_mom = gathered(times(m, code))
        coded_ref[4:8, lanes] = coded_grad
        coded_ref[0:4, lanes] = coded_mom
        rest_mom = decay_rate * (m - decode_block(coded_mom, wide_pick, decode))
        rest_grad = g.astype(f32) * (1 / SHIFT) - decode_block(coded_grad, pick, decode) * SHIFT
        for layer in range(layers):
            rest_mom_ref[0, layer, :, lanes] = rest_mom[layer * rows : (layer + 1) * rows]
            rest_grad_ref[0, layer, :, lanes] = rest_grad[layer * rows : (layer + 1) * rows]


def spectra_kernel(count, squares_ref, coded_ref, copies_ref, clip_ref):
    here = lax.axis_index("core")
    clips = []
    members = squares_ref.shape[0] // 2
    for core in range(2):
        total = jnp.sum(squares_ref[core * members : (core + 1) * members], axis=0)
        squares = [jnp.sum(total[i : i + 1], keepdims=True) for i in range(2)]
        square = jnp.concatenate([jnp.broadcast_to(s, (4, LANES)) for s in squares], axis=0)
        clips.append(1.0 / jnp.maximum(1.0, jnp.sqrt(square / count + epsilon)))
    clip_ref[...] = jnp.where(here == 0, clips[0], clips[1])
    for b in range(coded_ref.shape[2] // LANES):
        lanes = slice(b * LANES, (b + 1) * LANES)
        both = [decay_rate * coded_ref[core, 0:4, lanes] + clips[core][2:6] * coded_ref[core, 4:8, lanes] for core in range(2)]
        pair = both[0] + both[1]
        part = jnp.where(here == 0, pair[0:2], pair[2:4])
        copies_ref[:, :, lanes] = jnp.broadcast_to(part[None], (copies_ref.shape[0], 2, LANES))


def decode_block(spectra, pick, decode):
    return times((spectra[:, None, :] * pick[None]).reshape(-1, LANES), decode, transposed=True)


def last_kernel(rest_mom_ref, rest_grad_ref, clip_ref, total_ref, pick_ref, decode_ref, new_hbm, update_hbm, new_ref, update_ref, sems):
    layers, rows, cols = update_ref.shape
    copies = []
    for layer in range(layers):
        for b in range(cols // LANES):
            lanes = slice(b * LANES, (b + 1) * LANES)
            each = clip_ref[4 * layer : 4 * layer + 1, :]
            new_ref[0, layer, :, lanes] = rest_mom_ref[0, layer, :, lanes] + (each * rest_grad_ref[0, layer, :, lanes]) * SHIFT
        copies.append(pltpu.make_async_copy(new_ref.at[:, layer], new_hbm.at[:, layer], sems.at[layer]))
        copies[-1].start()
    lane = lax.broadcasted_iota(jnp.int32, (4, LANES), 1)
    for b in range(cols // LANES):
        lanes = slice(b * LANES, (b + 1) * LANES)
        tiles = decode_block(total_ref[:, lanes], pick_ref[...], decode_ref[...]).reshape(4, GROUP, LANES)
        size = jnp.sum(jnp.abs(tiles), axis=1)
        left = jnp.sum(jnp.where(lane < GROUP, size, 0.0), axis=1, keepdims=True)
        right = jnp.sum(jnp.where(lane < GROUP, 0.0, size), axis=1, keepdims=True)
        mean = jnp.where(lane < GROUP, left, right) / (GROUP * GROUP)
        scale = 1.0 / (mean + epsilon)
        update_ref[:, :, lanes] = jnp.tanh(tiles * scale[:, None, :]).astype(bf16).reshape(layers, rows, LANES)
        part = pl.ds(b * LANES, LANES)
        copies.append(pltpu.make_async_copy(update_ref.at[:, :, part], update_hbm.at[:, :, part], sems.at[layers + b]))
        copies[-1].start()
    for copy in copies:
        copy.wait()


def exchange(x, axes, groups):
    return lax.all_to_all(x, axes, 0, 0, axis_index_groups=groups, tiled=True)


def solution(mesh):
    whole = Mesh(mesh.devices.reshape(8, 4, 2, 2, 4), ("z", "yh", "core", "yl", "x"))
    rep, mp = ("z", "yh", "core"), ("yl", "x")

    first_groups = [[core * 8 + yl * 4 + (x + 2) % 4 for core in range(2) for yl in range(2) for x in range(4)]]
    second_groups = [
        [(((z + 6) % 8) * 4 + (yh + 2) % 4) * 2 + core for z in range(8) for yh in range(4)] for core in range(2)
    ]

    def per_device(momentum, gradient, kept_index):
        _, layers, rows, cols = momentum.shape
        count = float(rows * cols * 8)
        sds = jax.ShapeDtypeStruct

        shapes = (momentum.shape, f32), (gradient.shape, bf16), ((GROUP, LANES), f32), ((2 * LANES, 2 * LANES), bf16), ((2 * LANES, 2 * LANES), bf16)
        hbm = lambda x: pltpu.with_memory_space_constraint(x, pltpu.HBM)
        squares, momentum, gradient, pick, code, decode = pl.pallas_call(
            first_kernel,
            in_specs=[pl.BlockSpec(memory_space=pltpu.HBM)] * 3,
            out_shape=(pltpu.HBM((16, 2, LANES), f32), *[pltpu.VMEM(*s) for s in shapes]),
            out_specs=(pl.BlockSpec(memory_space=pltpu.HBM),) + (pl.BlockSpec(memory_space=pltpu.VMEM),) * 5,
            scratch_shapes=[
                pltpu.VMEM((16, 2, LANES), f32),
                pltpu.VMEM((1, GROUP), jnp.int32),
                pltpu.SemaphoreType.DMA((layers + 3,)),
            ],
            compiler_params=pltpu.CompilerParams(vmem_limit_bytes=24 * 1024 * 1024),
            name="squares",
        )(hbm(momentum), hbm(gradient), hbm(kept_index.reshape(1, GROUP)))
        squares = exchange(squares, ("core",) + mp, first_groups)
        vmem = lambda *shapes: tuple(pltpu.VMEM(*s) for s in shapes)
        room = pltpu.CompilerParams(vmem_limit_bytes=24 * 1024 * 1024)
        coded, rest_mom, rest_grad = pl.pallas_call(
            code_kernel,
            out_shape=vmem(((8, cols), f32), (momentum.shape, f32), (momentum.shape, f32)),
            out_specs=(pl.BlockSpec(memory_space=pltpu.VMEM),) * 3,
            compiler_params=room,
            cost_estimate=pl.CostEstimate(flops=1 << 28, bytes_accessed=1 << 22, transcendentals=0),
            name="transforms",
        )(momentum, gradient, pick, code, decode)
        coded = lax.all_gather(coded, "core")
        copies, clip = pl.pallas_call(
            lambda *refs: spectra_kernel(count, *refs),
            out_shape=vmem(((32, 2, cols), f32), ((8, LANES), f32)),
            out_specs=(pl.BlockSpec(memory_space=pltpu.VMEM),) * 2,
            compiler_params=room,
            name="spectra",
        )(squares, coded)
        got = exchange(copies, rep, second_groups)
        total = lax.all_gather(jnp.sum(got, axis=0), "core", tiled=True)
        return pl.pallas_call(
            last_kernel,
            out_shape=(pltpu.HBM(momentum.shape, f32), pltpu.HBM((layers, rows, cols), bf16)),
            out_specs=(pl.BlockSpec(memory_space=pltpu.HBM),) * 2,
            scratch_shapes=[
                pltpu.VMEM(momentum.shape, f32),
                pltpu.VMEM((layers, rows, cols), bf16),
                pltpu.SemaphoreType.DMA((layers + cols // LANES,)),
            ],
            compiler_params=room,
            name="new_momentum_and_update",
        )(rest_mom, rest_grad, clip, total, pick, decode)

    return jax.shard_map(
        per_device,
        mesh=whole,
        in_specs=(P(rep, None, None, mp), P(rep, None, None, mp), P()),
        out_specs=(P(rep, None, None, mp), P(None, None, mp)),
        check_vma=False,
    )
```

```python
import math

import jax
import jax.numpy as jnp
from jax import lax
from jax.experimental import pallas as pl
from jax.experimental.pallas import tpu as pltpu
from jax.sharding import Mesh, PartitionSpec as P

GROUP = 64
LANES = 128
decay_rate = 0.999
epsilon = 1e-06
f32 = jnp.float32
bf16 = jnp.bfloat16
SHIFT = 256.0


def kept_cosines(freq, place):
    turn = ((2 * place + 1) * freq) & 255
    turn = jnp.where(turn > 128, 256 - turn, turn)
    far = turn > 64
    angle = jnp.where(far, 128 - turn, turn).astype(f32) * (math.pi / 128)
    square = angle * angle
    series = jnp.full_like(square, 1 / math.factorial(12))
    for n in (10, 8, 6, 4, 2, 0):
        series = series * square + (1 if n % 4 == 0 else -1) / math.factorial(n)
    scale = jnp.where(freq == 0, math.sqrt(1.0 / GROUP), math.sqrt(2.0 / GROUP))
    return jnp.where(far, -series, series) * scale


def halves(x):
    high = x.astype(bf16)
    return high, (x - high.astype(f32)).astype(bf16)


def dot(a, b, transposed=False):
    dims = (((1,), (1 if transposed else 0,)), ((), ()))
    return lax.dot_general(a, b, dims, preferred_element_type=f32)


def times(x, wide, transposed=False):
    both = dot(jnp.concatenate(halves(x), axis=1), wide, transposed)
    return both[:, 0:LANES] + both[:, LANES : 2 * LANES]


def joined(high, low, transposed=False):
    zero = jnp.zeros_like(low)
    across, down = ((high, high), (low, zero)) if transposed else ((high, low), (high, zero))
    return jnp.concatenate([jnp.concatenate(across, axis=1), jnp.concatenate(down, axis=1)], axis=0)


def block(ref, b):
    lanes = slice(b * LANES, (b + 1) * LANES)
    return jnp.concatenate([ref[0, layer, :, lanes] for layer in range(ref.shape[1])], axis=0)


def first_kernel(mom_hbm, grad_hbm, kept_hbm, squares_hbm, mom_ref, grad_ref, pick_ref, code_ref, decode_ref, squares_ref, kept_ref, sems):
    layers = grad_ref.shape[1]
    copies = [pltpu.make_async_copy(grad_hbm.at[:, i], grad_ref.at[:, i], sems.at[i]) for i in range(layers)]
    copies += [pltpu.make_async_copy(kept_hbm, kept_ref, sems.at[layers])]
    copies += [pltpu.make_async_copy(mom_hbm, mom_ref, sems.at[layers + 1])]
    for copy in copies:
        copy.start()

    for layer in range(layers):
        copies[layer].wait()
        wide = grad_ref[0, layer].astype(f32)
        parts = jnp.sum((wide * wide).reshape(-1, 8, wide.shape[1]), axis=0)
        total = parts[:, 0:LANES]
        for b in range(1, wide.shape[1] // LANES):
            total = total + parts[:, b * LANES : (b + 1) * LANES]
        total = jnp.sum(total, axis=0, keepdims=True)
        squares_ref[:, layer : layer + 1] = jnp.broadcast_to(total[None], (squares_ref.shape[0], 1, LANES))
    out = pltpu.make_async_copy(squares_ref, squares_hbm, sems.at[layers + 2])
    out.start()

    copies[layers].wait()
    kept = kept_ref[...]
    kept = jnp.concatenate([kept, kept], axis=1)
    place = lax.broadcasted_iota(jnp.int32, (GROUP, LANES), 0)
    lane = lax.broadcasted_iota(jnp.int32, (GROUP, LANES), 1)
    pick_ref[...] = kept_cosines(kept >> 6, place) * (SHIFT * SHIFT)
    cols = kept_cosines(kept & 63, place) * (1 / SHIFT)
    both = jnp.concatenate([jnp.where(lane < GROUP, cols, 0.0), jnp.where(lane < GROUP, 0.0, cols)], axis=0)
    high, low = halves(both)
    code_ref[...] = joined(high, low)
    decode_ref[...] = joined(high, low, transposed=True)
    copies[-1].wait()
    out.wait()


def code_kernel(mom_ref, grad_ref, pick_ref, code_ref, decode_ref, coded_ref, rest_mom_ref, rest_grad_ref):
    layers, rows = grad_ref.shape[1:3]
    wide_pick = pick_ref[...]
    pick = wide_pick * (1 / (SHIFT * SHIFT))
    code, decode = code_ref[...], decode_ref[...]

    def gathered(t):
        return jnp.sum(t.reshape(-1, GROUP, LANES) * pick[None], axis=1)

    for b in range(grad_ref.shape[3] // LANES):
        lanes = slice(b * LANES, (b + 1) * LANES)
        g = block(grad_ref, b)
        t = dot(g, code[0:LANES])
        coded_grad = gathered(t[:, 0:LANES] + t[:, LANES : 2 * LANES])
        m = block(mom_ref, b)
        coded_mom = gathered(times(m, code))
        coded_ref[4:8, lanes] = coded_grad
        coded_ref[0:4, lanes] = coded_mom
        rest_mom = decay_rate * (m - decode_block(coded_mom, wide_pick, decode))
        rest_grad = g.astype(f32) * (1 / SHIFT) - decode_block(coded_grad, pick, decode) * SHIFT
        for layer in range(layers):
            rest_mom_ref[0, layer, :, lanes] = rest_mom[layer * rows : (layer + 1) * rows]
            rest_grad_ref[0, layer, :, lanes] = rest_grad[layer * rows : (layer + 1) * rows]


def spectra_kernel(count, squares_ref, coded_ref, copies_ref, clip_ref):
    here = lax.axis_index("core")
    clips = []
    members = squares_ref.shape[0] // 2
    for core in range(2):
        total = jnp.sum(squares_ref[core * members : (core + 1) * members], axis=0)
        squares = [jnp.sum(total[i : i + 1], keepdims=True) for i in range(2)]
        square = jnp.concatenate([jnp.broadcast_to(s, (4, LANES)) for s in squares], axis=0)
        clips.append(1.0 / jnp.maximum(1.0, jnp.sqrt(square / count + epsilon)))
    clip_ref[...] = jnp.where(here == 0, clips[0], clips[1])
    for b in range(coded_ref.shape[2] // LANES):
        lanes = slice(b * LANES, (b + 1) * LANES)
        both = [decay_rate * coded_ref[core, 0:4, lanes] + clips[core][2:6] * coded_ref[core, 4:8, lanes] for core in range(2)]
        pair = both[0] + both[1]
        part = jnp.where(here == 0, pair[0:2], pair[2:4])
        copies_ref[:, :, lanes] = jnp.broadcast_to(part[None], (copies_ref.shape[0], 2, LANES))


def decode_block(spectra, pick, decode):
    return times((spectra[:, None, :] * pick[None]).reshape(-1, LANES), decode, transposed=True)


def last_kernel(rest_mom_ref, rest_grad_ref, clip_ref, total_ref, pick_ref, decode_ref, new_hbm, update_hbm, new_ref, update_ref, sems):
    layers, rows, cols = update_ref.shape
    copies = []
    for layer in range(layers):
        for b in range(cols // LANES):
            lanes = slice(b * LANES, (b + 1) * LANES)
            each = clip_ref[4 * layer : 4 * layer + 1, :]
            new_ref[0, layer, :, lanes] = rest_mom_ref[0, layer, :, lanes] + (each * rest_grad_ref[0, layer, :, lanes]) * SHIFT
        copies.append(pltpu.make_async_copy(new_ref.at[:, layer], new_hbm.at[:, layer], sems.at[layer]))
        copies[-1].start()
    lane = lax.broadcasted_iota(jnp.int32, (4, LANES), 1)
    for b in range(cols // LANES):
        lanes = slice(b * LANES, (b + 1) * LANES)
        tiles = decode_block(total_ref[:, lanes], pick_ref[...], decode_ref[...]).reshape(4, GROUP, LANES)
        size = jnp.sum(jnp.abs(tiles), axis=1)
        left = jnp.sum(jnp.where(lane < GROUP, size, 0.0), axis=1, keepdims=True)
        right = jnp.sum(jnp.where(lane < GROUP, 0.0, size), axis=1, keepdims=True)
        mean = jnp.where(lane < GROUP, left, right) / (GROUP * GROUP)
        scale = 1.0 / (mean + epsilon)
        update_ref[:, :, lanes] = jnp.tanh(tiles * scale[:, None, :]).astype(bf16).reshape(layers, rows, LANES)
        part = pl.ds(b * LANES, LANES)
        copies.append(pltpu.make_async_copy(update_ref.at[:, :, part], update_hbm.at[:, :, part], sems.at[layers + b]))
        copies[-1].start()
    for copy in copies:
        copy.wait()


def exchange(x, axes, groups):
    return lax.all_to_all(x, axes, 0, 0, axis_index_groups=groups, tiled=True)


def solution(mesh):
    whole = Mesh(mesh.devices.reshape(8, 4, 2, 2, 4), ("z", "yh", "core", "yl", "x"))
    rep, mp = ("z", "yh", "core"), ("yl", "x")

    first_groups = [[core * 8 + yl * 4 + (x + 2) % 4 for core in range(2) for yl in range(2) for x in range(4)]]
    second_groups = [
        [(((z + 6) % 8) * 4 + (yh + 2) % 4) * 2 + core for z in range(8) for yh in range(4)] for core in range(2)
    ]

    def per_device(momentum, gradient, kept_index):
        _, layers, rows, cols = momentum.shape
        count = float(rows * cols * 8)
        sds = jax.ShapeDtypeStruct

        shapes = (momentum.shape, f32), (gradient.shape, bf16), ((GROUP, LANES), f32), ((2 * LANES, 2 * LANES), bf16), ((2 * LANES, 2 * LANES), bf16)
        hbm = lambda x: pltpu.with_memory_space_constraint(x, pltpu.HBM)
        squares, momentum, gradient, pick, code, decode = pl.pallas_call(
            first_kernel,
            in_specs=[pl.BlockSpec(memory_space=pltpu.HBM)] * 3,
            out_shape=(pltpu.HBM((16, 2, LANES), f32), *[pltpu.VMEM(*s) for s in shapes]),
            out_specs=(pl.BlockSpec(memory_space=pltpu.HBM),) + (pl.BlockSpec(memory_space=pltpu.VMEM),) * 5,
            scratch_shapes=[
                pltpu.VMEM((16, 2, LANES), f32),
                pltpu.VMEM((1, GROUP), jnp.int32),
                pltpu.SemaphoreType.DMA((layers + 3,)),
            ],
            compiler_params=pltpu.CompilerParams(vmem_limit_bytes=24 * 1024 * 1024),
            name="squares",
        )(hbm(momentum), hbm(gradient), hbm(kept_index.reshape(1, GROUP)))
        squares = exchange(squares, ("core",) + mp, first_groups)
        vmem = lambda *shapes: tuple(pltpu.VMEM(*s) for s in shapes)
        room = pltpu.CompilerParams(vmem_limit_bytes=24 * 1024 * 1024)
        coded, rest_mom, rest_grad = pl.pallas_call(
            code_kernel,
            out_shape=vmem(((8, cols), f32), (momentum.shape, f32), (momentum.shape, f32)),
            out_specs=(pl.BlockSpec(memory_space=pltpu.VMEM),) * 3,
            compiler_params=room,
            cost_estimate=pl.CostEstimate(flops=1 << 28, bytes_accessed=1 << 22, transcendentals=0),
            name="transforms",
        )(momentum, gradient, pick, code, decode)
        coded = lax.all_gather(coded, "core")
        copies, clip = pl.pallas_call(
            lambda *refs: spectra_kernel(count, *refs),
            out_shape=vmem(((32, 2, cols), f32), ((8, LANES), f32)),
            out_specs=(pl.BlockSpec(memory_space=pltpu.VMEM),) * 2,
            compiler_params=room,
            name="spectra",
        )(squares, coded)
        got = exchange(copies, rep, second_groups)
        total = lax.all_gather(jnp.sum(got, axis=0), "core", tiled=True)
        return pl.pallas_call(
            last_kernel,
            out_shape=(pltpu.HBM(momentum.shape, f32), pltpu.HBM((layers, rows, cols), bf16)),
            out_specs=(pl.BlockSpec(memory_space=pltpu.HBM),) * 2,
            scratch_shapes=[
                pltpu.VMEM(momentum.shape, f32),
                pltpu.VMEM((layers, rows, cols), bf16),
                pltpu.SemaphoreType.DMA((layers + cols // LANES,)),
            ],
            compiler_params=room,
            name="new_momentum_and_update",
        )(rest_mom, rest_grad, clip, total, pick, decode)

    return jax.shard_map(
        per_device,
        mesh=whole,
        in_specs=(P(rep, None, None, mp), P(rep, None, None, mp), P()),
        out_specs=(P(rep, None, None, mp), P(None, None, mp)),
        check_vma=False,
    )
```

```python
import math

import jax
import jax.numpy as jnp
from jax import lax
from jax.experimental import pallas as pl
from jax.experimental.pallas import tpu as pltpu
from jax.sharding import Mesh, PartitionSpec as P

GROUP = 64
LANES = 128
CHUNK = 32
decay_rate = 0.999
epsilon = 1e-06
f32 = jnp.float32
bf16 = jnp.bfloat16
SHIFT = 256.0


def kept_cosines(freq, place):
    turn = ((2 * place + 1) * freq) & 255
    turn = jnp.where(turn > 128, 256 - turn, turn)
    far = turn > 64
    angle = jnp.where(far, 128 - turn, turn).astype(f32) * (math.pi / 128)
    square = angle * angle
    series = jnp.full_like(square, 1 / math.factorial(12))
    for n in (10, 8, 6, 4, 2, 0):
        series = series * square + (1 if n % 4 == 0 else -1) / math.factorial(n)
    scale = jnp.where(freq == 0, math.sqrt(1.0 / GROUP), math.sqrt(2.0 / GROUP))
    return jnp.where(far, -series, series) * scale


def halves(x):
    high = x.astype(bf16)
    return high, (x - high.astype(f32)).astype(bf16)


def dot(a, b, transposed=False):
    dims = (((1,), (1 if transposed else 0,)), ((), ()))
    return lax.dot_general(a, b, dims, preferred_element_type=f32)


def times(x, wide, transposed=False):
    both = dot(jnp.concatenate(halves(x), axis=1), wide, transposed)
    return both[:, 0:LANES] + both[:, LANES : 2 * LANES]


def joined(high, low, transposed=False):
    zero = jnp.zeros_like(low)
    across, down = ((high, high), (low, zero)) if transposed else ((high, low), (high, zero))
    return jnp.concatenate([jnp.concatenate(across, axis=1), jnp.concatenate(down, axis=1)], axis=0)


def block(ref, b):
    lanes = slice(b * LANES, (b + 1) * LANES)
    return jnp.concatenate([ref[0, layer, :, lanes] for layer in range(ref.shape[1])], axis=0)


def first_kernel(mom_hbm, grad_hbm, kept_hbm, squares_hbm, mom_ref, grad_ref, pick_ref, code_ref, decode_ref, squares_ref, kept_ref, sems):
    layers = grad_ref.shape[1]
    copies = [pltpu.make_async_copy(grad_hbm.at[:, i], grad_ref.at[:, i], sems.at[i]) for i in range(layers)]
    copies += [pltpu.make_async_copy(kept_hbm, kept_ref, sems.at[layers])]
    copies += [pltpu.make_async_copy(mom_hbm, mom_ref, sems.at[layers + 1])]
    for copy in copies:
        copy.start()

    for layer in range(layers):
        copies[layer].wait()
        wide = grad_ref[0, layer].astype(f32)
        parts = jnp.sum((wide * wide).reshape(-1, 8, wide.shape[1]), axis=0)
        total = parts[:, 0:LANES]
        for b in range(1, wide.shape[1] // LANES):
            total = total + parts[:, b * LANES : (b + 1) * LANES]
        total = jnp.sum(total, axis=0, keepdims=True)
        squares_ref[:, layer : layer + 1] = jnp.broadcast_to(total[None], (squares_ref.shape[0], 1, LANES))
    out = pltpu.make_async_copy(squares_ref, squares_hbm, sems.at[layers + 2])
    out.start()

    copies[layers].wait()
    kept = kept_ref[...]
    kept = jnp.concatenate([kept, kept], axis=1)
    place = lax.broadcasted_iota(jnp.int32, (GROUP, LANES), 0)
    lane = lax.broadcasted_iota(jnp.int32, (GROUP, LANES), 1)
    pick_ref[...] = kept_cosines(kept >> 6, place) * (SHIFT * SHIFT)
    cols = kept_cosines(kept & 63, place) * (1 / SHIFT)
    both = jnp.concatenate([jnp.where(lane < GROUP, cols, 0.0), jnp.where(lane < GROUP, 0.0, cols)], axis=0)
    high, low = halves(both)
    code_ref[...] = joined(high, low)
    decode_ref[...] = joined(high, low, transposed=True)
    copies[-1].wait()
    out.wait()


def code_kernel(mom_ref, grad_ref, pick_ref, code_ref, decode_ref, coded_ref, rest_mom_ref, rest_grad_ref):
    layers, rows = grad_ref.shape[1:3]
    wide_pick = pick_ref[...]
    pick = wide_pick * (1 / (SHIFT * SHIFT))
    code, decode = code_ref[...], decode_ref[...]

    def gathered(t):
        return jnp.sum(t.reshape(-1, GROUP, LANES) * pick[None], axis=1)

    for b in range(grad_ref.shape[3] // LANES):
        lanes = slice(b * LANES, (b + 1) * LANES)
        g = block(grad_ref, b)
        t = dot(g, code[0:LANES])
        coded_grad = gathered(t[:, 0:LANES] + t[:, LANES : 2 * LANES])
        m = block(mom_ref, b)
        coded_mom = gathered(times(m, code))
        coded_ref[4:8, lanes] = coded_grad
        coded_ref[0:4, lanes] = coded_mom
        rest_mom = decay_rate * (m - decode_block(coded_mom, wide_pick, decode))
        rest_grad = g.astype(f32) * (1 / SHIFT) - decode_block(coded_grad, pick, decode) * SHIFT
        for layer in range(layers):
            rest_mom_ref[0, layer, :, lanes] = rest_mom[layer * rows : (layer + 1) * rows]
            rest_grad_ref[0, layer, :, lanes] = rest_grad[layer * rows : (layer + 1) * rows]


def spectra_kernel(count, squares_ref, coded_ref, copies_ref, clip_ref):
    here = lax.axis_index("core")
    clips = []
    members = squares_ref.shape[0] // 2
    for core in range(2):
        total = jnp.sum(squares_ref[core * members : (core + 1) * members], axis=0)
        squares = [jnp.sum(total[i : i + 1], keepdims=True) for i in range(2)]
        square = jnp.concatenate([jnp.broadcast_to(s, (4, LANES)) for s in squares], axis=0)
        clips.append(1.0 / jnp.maximum(1.0, jnp.sqrt(square / count + epsilon)))
    clip_ref[...] = jnp.where(here == 0, clips[0], clips[1])
    for b in range(coded_ref.shape[2] // LANES):
        lanes = slice(b * LANES, (b + 1) * LANES)
        both = [decay_rate * coded_ref[core, 0:4, lanes] + clips[core][2:6] * coded_ref[core, 4:8, lanes] for core in range(2)]
        pair = both[0] + both[1]
        part = jnp.where(here == 0, pair[0:2], pair[2:4])
        copies_ref[:, :, lanes] = jnp.broadcast_to(part[None], (copies_ref.shape[0], 2, LANES))


def decode_block(spectra, pick, decode):
    return times((spectra[:, None, :] * pick[None]).reshape(-1, LANES), decode, transposed=True)


def last_kernel(rest_mom_ref, rest_grad_ref, clip_ref, total_ref, pick_ref, decode_ref, new_hbm, update_hbm, new_ref, update_ref, sems):
    layers, rows, cols = update_ref.shape
    copies = []
    for layer in range(layers):
        each = clip_ref[4 * layer : 4 * layer + 1, :]
        for start in range(0, rows, CHUNK):
            part = pl.ds(start, CHUNK)
            for b in range(cols // LANES):
                lanes = pl.ds(b * LANES, LANES)
                new_ref[0, layer, part, lanes] = rest_mom_ref[0, layer, part, lanes] + (each * rest_grad_ref[0, layer, part, lanes]) * SHIFT
            copies.append(pltpu.make_async_copy(new_ref.at[:, layer, part], new_hbm.at[:, layer, part], sems.at[len(copies)]))
            copies[-1].start()
    lane = lax.broadcasted_iota(jnp.int32, (4, LANES), 1)
    for b in range(cols // LANES):
        lanes = slice(b * LANES, (b + 1) * LANES)
        tiles = decode_block(total_ref[:, lanes], pick_ref[...], decode_ref[...]).reshape(4, GROUP, LANES)
        size = jnp.sum(jnp.abs(tiles), axis=1)
        left = jnp.sum(jnp.where(lane < GROUP, size, 0.0), axis=1, keepdims=True)
        right = jnp.sum(jnp.where(lane < GROUP, 0.0, size), axis=1, keepdims=True)
        mean = jnp.where(lane < GROUP, left, right) / (GROUP * GROUP)
        scale = 1.0 / (mean + epsilon)
        update_ref[:, :, lanes] = jnp.tanh(tiles * scale[:, None, :]).astype(bf16).reshape(layers, rows, LANES)
        part = pl.ds(b * LANES, LANES)
        copies.append(pltpu.make_async_copy(update_ref.at[:, :, part], update_hbm.at[:, :, part], sems.at[len(copies)]))
        copies[-1].start()
    for copy in copies:
        copy.wait()


def exchange(x, axes, groups):
    return lax.all_to_all(x, axes, 0, 0, axis_index_groups=groups, tiled=True)


def solution(mesh):
    whole = Mesh(mesh.devices.reshape(8, 4, 2, 2, 4), ("z", "yh", "core", "yl", "x"))
    rep, mp = ("z", "yh", "core"), ("yl", "x")

    first_groups = [[core * 8 + yl * 4 + (x + 2) % 4 for core in range(2) for yl in range(2) for x in range(4)]]
    second_groups = [
        [(((z + 6) % 8) * 4 + (yh + 2) % 4) * 2 + core for z in range(8) for yh in range(4)] for core in range(2)
    ]

    def per_device(momentum, gradient, kept_index):
        _, layers, rows, cols = momentum.shape
        count = float(rows * cols * 8)
        sds = jax.ShapeDtypeStruct

        shapes = (momentum.shape, f32), (gradient.shape, bf16), ((GROUP, LANES), f32), ((2 * LANES, 2 * LANES), bf16), ((2 * LANES, 2 * LANES), bf16)
        hbm = lambda x: pltpu.with_memory_space_constraint(x, pltpu.HBM)
        squares, momentum, gradient, pick, code, decode = pl.pallas_call(
            first_kernel,
            in_specs=[pl.BlockSpec(memory_space=pltpu.HBM)] * 3,
            out_shape=(pltpu.HBM((16, 2, LANES), f32), *[pltpu.VMEM(*s) for s in shapes]),
            out_specs=(pl.BlockSpec(memory_space=pltpu.HBM),) + (pl.BlockSpec(memory_space=pltpu.VMEM),) * 5,
            scratch_shapes=[
                pltpu.VMEM((16, 2, LANES), f32),
                pltpu.VMEM((1, GROUP), jnp.int32),
                pltpu.SemaphoreType.DMA((layers + 3,)),
            ],
            compiler_params=pltpu.CompilerParams(vmem_limit_bytes=24 * 1024 * 1024),
            name="squares",
        )(hbm(momentum), hbm(gradient), hbm(kept_index.reshape(1, GROUP)))
        squares = exchange(squares, ("core",) + mp, first_groups)
        vmem = lambda *shapes: tuple(pltpu.VMEM(*s) for s in shapes)
        room = pltpu.CompilerParams(vmem_limit_bytes=24 * 1024 * 1024)
        coded, rest_mom, rest_grad = pl.pallas_call(
            code_kernel,
            out_shape=vmem(((8, cols), f32), (momentum.shape, f32), (momentum.shape, f32)),
            out_specs=(pl.BlockSpec(memory_space=pltpu.VMEM),) * 3,
            compiler_params=room,
            cost_estimate=pl.CostEstimate(flops=1 << 28, bytes_accessed=1 << 22, transcendentals=0),
            name="transforms",
        )(momentum, gradient, pick, code, decode)
        coded = lax.all_gather(coded, "core")
        copies, clip = pl.pallas_call(
            lambda *refs: spectra_kernel(count, *refs),
            out_shape=vmem(((32, 2, cols), f32), ((8, LANES), f32)),
            out_specs=(pl.BlockSpec(memory_space=pltpu.VMEM),) * 2,
            compiler_params=room,
            name="spectra",
        )(squares, coded)
        got = exchange(copies, rep, second_groups)
        total = lax.all_gather(jnp.sum(got, axis=0), "core", tiled=True)
        return pl.pallas_call(
            last_kernel,
            out_shape=(pltpu.HBM(momentum.shape, f32), pltpu.HBM((layers, rows, cols), bf16)),
            out_specs=(pl.BlockSpec(memory_space=pltpu.HBM),) * 2,
            scratch_shapes=[
                pltpu.VMEM(momentum.shape, f32),
                pltpu.VMEM((layers, rows, cols), bf16),
                pltpu.SemaphoreType.DMA((layers * (rows // CHUNK) + cols // LANES,)),
            ],
            compiler_params=room,
            name="new_momentum_and_update",
        )(rest_mom, rest_grad, clip, total, pick, decode)

    return jax.shard_map(
        per_device,
        mesh=whole,
        in_specs=(P(rep, None, None, mp), P(rep, None, None, mp), P()),
        out_specs=(P(rep, None, None, mp), P(None, None, mp)),
        check_vma=False,
    )
```

```python
import math

import jax
import jax.numpy as jnp
from jax import lax
from jax.experimental import pallas as pl
from jax.experimental.pallas import tpu as pltpu
from jax.sharding import Mesh, PartitionSpec as P

GROUP = 64
LANES = 128
CHUNK = 32
decay_rate = 0.999
epsilon = 1e-06
f32 = jnp.float32
bf16 = jnp.bfloat16
SHIFT = 256.0


def kept_cosines(freq, place):
    turn = ((2 * place + 1) * freq) & 255
    turn = jnp.where(turn > 128, 256 - turn, turn)
    far = turn > 64
    angle = jnp.where(far, 128 - turn, turn).astype(f32) * (math.pi / 128)
    square = angle * angle
    series = jnp.full_like(square, 1 / math.factorial(12))
    for n in (10, 8, 6, 4, 2, 0):
        series = series * square + (1 if n % 4 == 0 else -1) / math.factorial(n)
    scale = jnp.where(freq == 0, math.sqrt(1.0 / GROUP), math.sqrt(2.0 / GROUP))
    return jnp.where(far, -series, series) * scale


def halves(x):
    high = x.astype(bf16)
    return high, (x - high.astype(f32)).astype(bf16)


def dot(a, b, transposed=False):
    dims = (((1,), (1 if transposed else 0,)), ((), ()))
    return lax.dot_general(a, b, dims, preferred_element_type=f32)


def times(x, wide, transposed=False):
    both = dot(jnp.concatenate(halves(x), axis=1), wide, transposed)
    return both[:, 0:LANES] + both[:, LANES : 2 * LANES]


def joined(high, low, transposed=False):
    zero = jnp.zeros_like(low)
    across, down = ((high, high), (low, zero)) if transposed else ((high, low), (high, zero))
    return jnp.concatenate([jnp.concatenate(across, axis=1), jnp.concatenate(down, axis=1)], axis=0)


def block(ref, b):
    lanes = slice(b * LANES, (b + 1) * LANES)
    return jnp.concatenate([ref[0, layer, :, lanes] for layer in range(ref.shape[1])], axis=0)


def first_kernel(mom_hbm, grad_hbm, kept_hbm, squares_hbm, mom_ref, grad_ref, pick_ref, code_ref, decode_ref, squares_ref, kept_ref, sems):
    layers = grad_ref.shape[1]
    half = grad_ref.shape[2] // 2
    copies = []
    for i in range(2 * layers):
        part = (slice(None), i // 2, pl.ds(i % 2 * half, half))
        copies.append(pltpu.make_async_copy(grad_hbm.at[part], grad_ref.at[part], sems.at[i]))
    copies += [pltpu.make_async_copy(kept_hbm, kept_ref, sems.at[2 * layers])]
    copies += [pltpu.make_async_copy(mom_hbm, mom_ref, sems.at[2 * layers + 1])]
    for copy in copies:
        copy.start()

    for layer in range(layers):
        parts = 0.0
        for i in range(2):
            copies[2 * layer + i].wait()
            wide = grad_ref[0, layer, i * half : (i + 1) * half].astype(f32)
            parts = parts + jnp.sum((wide * wide).reshape(-1, 8, wide.shape[1]), axis=0)
        total = parts[:, 0:LANES]
        for b in range(1, wide.shape[1] // LANES):
            total = total + parts[:, b * LANES : (b + 1) * LANES]
        total = jnp.sum(total, axis=0, keepdims=True)
        squares_ref[:, layer : layer + 1] = jnp.broadcast_to(total[None], (squares_ref.shape[0], 1, LANES))
    out = pltpu.make_async_copy(squares_ref, squares_hbm, sems.at[2 * layers + 2])
    out.start()

    copies[2 * layers].wait()
    kept = kept_ref[...]
    kept = jnp.concatenate([kept, kept], axis=1)
    place = lax.broadcasted_iota(jnp.int32, (GROUP, LANES), 0)
    lane = lax.broadcasted_iota(jnp.int32, (GROUP, LANES), 1)
    pick_ref[...] = kept_cosines(kept >> 6, place) * (SHIFT * SHIFT)
    cols = kept_cosines(kept & 63, place) * (1 / SHIFT)
    both = jnp.concatenate([jnp.where(lane < GROUP, cols, 0.0), jnp.where(lane < GROUP, 0.0, cols)], axis=0)
    high, low = halves(both)
    code_ref[...] = joined(high, low)
    decode_ref[...] = joined(high, low, transposed=True)
    copies[-1].wait()
    out.wait()


def code_kernel(mom_ref, grad_ref, pick_ref, code_ref, decode_ref, coded_ref, rest_mom_ref, rest_grad_ref):
    layers, rows = grad_ref.shape[1:3]
    wide_pick = pick_ref[...]
    pick = wide_pick * (1 / (SHIFT * SHIFT))
    code, decode = code_ref[...], decode_ref[...]

    def gathered(t):
        return jnp.sum(t.reshape(-1, GROUP, LANES) * pick[None], axis=1)

    for b in range(grad_ref.shape[3] // LANES):
        lanes = slice(b * LANES, (b + 1) * LANES)
        g = block(grad_ref, b)
        t = dot(g, code[0:LANES])
        coded_grad = gathered(t[:, 0:LANES] + t[:, LANES : 2 * LANES])
        m = block(mom_ref, b)
        coded_mom = gathered(times(m, code))
        coded_ref[4:8, lanes] = coded_grad
        coded_ref[0:4, lanes] = coded_mom
        rest_mom = decay_rate * (m - decode_block(coded_mom, wide_pick, decode))
        rest_grad = g.astype(f32) * (1 / SHIFT) - decode_block(coded_grad, pick, decode) * SHIFT
        for layer in range(layers):
            rest_mom_ref[0, layer, :, lanes] = rest_mom[layer * rows : (layer + 1) * rows]
            rest_grad_ref[0, layer, :, lanes] = rest_grad[layer * rows : (layer + 1) * rows]


def spectra_kernel(count, squares_ref, coded_ref, copies_ref, clip_ref):
    here = lax.axis_index("core")
    clips = []
    members = squares_ref.shape[0] // 2
    for core in range(2):
        total = jnp.sum(squares_ref[core * members : (core + 1) * members], axis=0)
        squares = [jnp.sum(total[i : i + 1], keepdims=True) for i in range(2)]
        square = jnp.concatenate([jnp.broadcast_to(s, (4, LANES)) for s in squares], axis=0)
        clips.append(1.0 / jnp.maximum(1.0, jnp.sqrt(square / count + epsilon)))
    clip_ref[...] = jnp.where(here == 0, clips[0], clips[1])
    for b in range(coded_ref.shape[2] // LANES):
        lanes = slice(b * LANES, (b + 1) * LANES)
        both = [decay_rate * coded_ref[core, 0:4, lanes] + clips[core][2:6] * coded_ref[core, 4:8, lanes] for core in range(2)]
        pair = both[0] + both[1]
        part = jnp.where(here == 0, pair[0:2], pair[2:4])
        copies_ref[:, :, lanes] = jnp.broadcast_to(part[None], (copies_ref.shape[0], 2, LANES))


def decode_block(spectra, pick, decode):
    return times((spectra[:, None, :] * pick[None]).reshape(-1, LANES), decode, transposed=True)


def last_kernel(rest_mom_ref, rest_grad_ref, clip_ref, total_ref, pick_ref, decode_ref, new_hbm, update_hbm, new_ref, update_ref, sems):
    layers, rows, cols = update_ref.shape
    copies = []
    for layer in range(layers):
        each = clip_ref[4 * layer : 4 * layer + 1, :]
        for start in range(0, rows, CHUNK):
            part = pl.ds(start, CHUNK)
            for b in range(cols // LANES):
                lanes = pl.ds(b * LANES, LANES)
                new_ref[0, layer, part, lanes] = rest_mom_ref[0, layer, part, lanes] + (each * rest_grad_ref[0, layer, part, lanes]) * SHIFT
            copies.append(pltpu.make_async_copy(new_ref.at[:, layer, part], new_hbm.at[:, layer, part], sems.at[len(copies)]))
            copies[-1].start()
    lane = lax.broadcasted_iota(jnp.int32, (4, LANES), 1)
    for b in range(cols // LANES):
        lanes = slice(b * LANES, (b + 1) * LANES)
        tiles = decode_block(total_ref[:, lanes], pick_ref[...], decode_ref[...]).reshape(4, GROUP, LANES)
        size = jnp.sum(jnp.abs(tiles), axis=1)
        left = jnp.sum(jnp.where(lane < GROUP, size, 0.0), axis=1, keepdims=True)
        right = jnp.sum(jnp.where(lane < GROUP, 0.0, size), axis=1, keepdims=True)
        mean = jnp.where(lane < GROUP, left, right) / (GROUP * GROUP)
        scale = 1.0 / (mean + epsilon)
        update_ref[:, :, lanes] = jnp.tanh(tiles * scale[:, None, :]).astype(bf16).reshape(layers, rows, LANES)
        part = pl.ds(b * LANES, LANES)
        copies.append(pltpu.make_async_copy(update_ref.at[:, :, part], update_hbm.at[:, :, part], sems.at[len(copies)]))
        copies[-1].start()
    for copy in copies:
        copy.wait()


def exchange(x, axes, groups):
    return lax.all_to_all(x, axes, 0, 0, axis_index_groups=groups, tiled=True)


def solution(mesh):
    whole = Mesh(mesh.devices.reshape(8, 4, 2, 2, 4), ("z", "yh", "core", "yl", "x"))
    rep, mp = ("z", "yh", "core"), ("yl", "x")

    first_groups = [[core * 8 + yl * 4 + (x + 2) % 4 for core in range(2) for yl in range(2) for x in range(4)]]
    second_groups = [
        [(((z + 6) % 8) * 4 + (yh + 2) % 4) * 2 + core for z in range(8) for yh in range(4)] for core in range(2)
    ]

    def per_device(momentum, gradient, kept_index):
        _, layers, rows, cols = momentum.shape
        count = float(rows * cols * 8)
        sds = jax.ShapeDtypeStruct

        shapes = (momentum.shape, f32), (gradient.shape, bf16), ((GROUP, LANES), f32), ((2 * LANES, 2 * LANES), bf16), ((2 * LANES, 2 * LANES), bf16)
        hbm = lambda x: pltpu.with_memory_space_constraint(x, pltpu.HBM)
        squares, momentum, gradient, pick, code, decode = pl.pallas_call(
            first_kernel,
            in_specs=[pl.BlockSpec(memory_space=pltpu.HBM)] * 3,
            out_shape=(pltpu.HBM((16, 2, LANES), f32), *[pltpu.VMEM(*s) for s in shapes]),
            out_specs=(pl.BlockSpec(memory_space=pltpu.HBM),) + (pl.BlockSpec(memory_space=pltpu.VMEM),) * 5,
            scratch_shapes=[
                pltpu.VMEM((16, 2, LANES), f32),
                pltpu.VMEM((1, GROUP), jnp.int32),
                pltpu.SemaphoreType.DMA((2 * layers + 3,)),
            ],
            compiler_params=pltpu.CompilerParams(vmem_limit_bytes=24 * 1024 * 1024),
            name="squares",
        )(hbm(momentum), hbm(gradient), hbm(kept_index.reshape(1, GROUP)))
        squares = exchange(squares, ("core",) + mp, first_groups)
        vmem = lambda *shapes: tuple(pltpu.VMEM(*s) for s in shapes)
        room = pltpu.CompilerParams(vmem_limit_bytes=24 * 1024 * 1024)
        coded, rest_mom, rest_grad = pl.pallas_call(
            code_kernel,
            out_shape=vmem(((8, cols), f32), (momentum.shape, f32), (momentum.shape, f32)),
            out_specs=(pl.BlockSpec(memory_space=pltpu.VMEM),) * 3,
            compiler_params=room,
            cost_estimate=pl.CostEstimate(flops=1 << 28, bytes_accessed=1 << 22, transcendentals=0),
            name="transforms",
        )(momentum, gradient, pick, code, decode)
        coded = lax.all_gather(coded, "core")
        copies, clip = pl.pallas_call(
            lambda *refs: spectra_kernel(count, *refs),
            out_shape=vmem(((32, 2, cols), f32), ((8, LANES), f32)),
            out_specs=(pl.BlockSpec(memory_space=pltpu.VMEM),) * 2,
            compiler_params=room,
            name="spectra",
        )(squares, coded)
        got = exchange(copies, rep, second_groups)
        total = lax.all_gather(jnp.sum(got, axis=0), "core", tiled=True)
        return pl.pallas_call(
            last_kernel,
            out_shape=(pltpu.HBM(momentum.shape, f32), pltpu.HBM((layers, rows, cols), bf16)),
            out_specs=(pl.BlockSpec(memory_space=pltpu.HBM),) * 2,
            scratch_shapes=[
                pltpu.VMEM(momentum.shape, f32),
                pltpu.VMEM((layers, rows, cols), bf16),
                pltpu.SemaphoreType.DMA((layers * (rows // CHUNK) + cols // LANES,)),
            ],
            compiler_params=room,
            name="new_momentum_and_update",
        )(rest_mom, rest_grad, clip, total, pick, decode)

    return jax.shard_map(
        per_device,
        mesh=whole,
        in_specs=(P(rep, None, None, mp), P(rep, None, None, mp), P()),
        out_specs=(P(rep, None, None, mp), P(None, None, mp)),
        check_vma=False,
    )
```

```python
import math

import jax
import jax.numpy as jnp
from jax import lax
from jax.experimental import pallas as pl
from jax.experimental.pallas import tpu as pltpu
from jax.sharding import Mesh, PartitionSpec as P

GROUP = 64
LANES = 128
decay_rate = 0.999
epsilon = 1e-06
f32 = jnp.float32
bf16 = jnp.bfloat16
SHIFT = 256.0


def kept_cosines(freq, place):
    turn = ((2 * place + 1) * freq) & 255
    turn = jnp.where(turn > 128, 256 - turn, turn)
    far = turn > 64
    angle = jnp.where(far, 128 - turn, turn).astype(f32) * (math.pi / 128)
    square = angle * angle
    series = jnp.full_like(square, 1 / math.factorial(12))
    for n in (10, 8, 6, 4, 2, 0):
        series = series * square + (1 if n % 4 == 0 else -1) / math.factorial(n)
    scale = jnp.where(freq == 0, math.sqrt(1.0 / GROUP), math.sqrt(2.0 / GROUP))
    return jnp.where(far, -series, series) * scale


def halves(x):
    high = x.astype(bf16)
    return high, (x - high.astype(f32)).astype(bf16)


def dot(a, b, transposed=False):
    dims = (((1,), (1 if transposed else 0,)), ((), ()))
    return lax.dot_general(a, b, dims, preferred_element_type=f32)


def times(x, wide, transposed=False):
    both = dot(jnp.concatenate(halves(x), axis=1), wide, transposed)
    return both[:, 0:LANES] + both[:, LANES : 2 * LANES]


def joined(high, low, transposed=False):
    zero = jnp.zeros_like(low)
    across, down = ((high, high), (low, zero)) if transposed else ((high, low), (high, zero))
    return jnp.concatenate([jnp.concatenate(across, axis=1), jnp.concatenate(down, axis=1)], axis=0)


def block(ref, b):
    lanes = slice(b * LANES, (b + 1) * LANES)
    return jnp.concatenate([ref[0, layer, :, lanes] for layer in range(ref.shape[1])], axis=0)


def first_kernel(mom_hbm, grad_hbm, kept_hbm, squares_hbm, mom_ref, grad_ref, pick_ref, code_ref, decode_ref, squares_ref, kept_ref, sems):
    layers = grad_ref.shape[1]
    copies = [pltpu.make_async_copy(grad_hbm.at[:, i], grad_ref.at[:, i], sems.at[i]) for i in range(layers)]
    copies += [pltpu.make_async_copy(kept_hbm, kept_ref, sems.at[layers])]
    copies += [pltpu.make_async_copy(mom_hbm, mom_ref, sems.at[layers + 1])]
    for copy in copies:
        copy.start()

    for layer in range(layers):
        copies[layer].wait()
        wide = grad_ref[0, layer].astype(f32)
        parts = jnp.sum((wide * wide).reshape(-1, 8, wide.shape[1]), axis=0)
        total = parts[:, 0:LANES]
        for b in range(1, wide.shape[1] // LANES):
            total = total + parts[:, b * LANES : (b + 1) * LANES]
        total = jnp.sum(total, axis=0, keepdims=True)
        squares_ref[:, layer : layer + 1] = jnp.broadcast_to(total[None], (squares_ref.shape[0], 1, LANES))
    out = pltpu.make_async_copy(squares_ref, squares_hbm, sems.at[layers + 2])
    out.start()

    copies[layers].wait()
    kept = kept_ref[...]
    kept = jnp.concatenate([kept, kept], axis=1)
    place = lax.broadcasted_iota(jnp.int32, (GROUP, LANES), 0)
    lane = lax.broadcasted_iota(jnp.int32, (GROUP, LANES), 1)
    pick_ref[...] = kept_cosines(kept >> 6, place) * (SHIFT * SHIFT)
    cols = kept_cosines(kept & 63, place) * (1 / SHIFT)
    both = jnp.concatenate([jnp.where(lane < GROUP, cols, 0.0), jnp.where(lane < GROUP, 0.0, cols)], axis=0)
    high, low = halves(both)
    code_ref[...] = joined(high, low)
    decode_ref[...] = joined(high, low, transposed=True)
    copies[-1].wait()
    out.wait()


def code_kernel(mom_ref, grad_ref, pick_ref, code_ref, decode_ref, coded_ref, rest_mom_ref, rest_grad_ref):
    layers, rows = grad_ref.shape[1:3]
    wide_pick = pick_ref[...]
    pick = wide_pick * (1 / (SHIFT * SHIFT))
    code, decode = code_ref[...], decode_ref[...]

    def gathered(t):
        return jnp.sum(t.reshape(-1, GROUP, LANES) * pick[None], axis=1)

    for b in range(grad_ref.shape[3] // LANES):
        lanes = slice(b * LANES, (b + 1) * LANES)
        g = block(grad_ref, b)
        t = dot(g, code[0:LANES])
        coded_grad = gathered(t[:, 0:LANES] + t[:, LANES : 2 * LANES])
        m = block(mom_ref, b)
        coded_mom = gathered(times(m, code))
        coded_ref[4:8, lanes] = coded_grad
        coded_ref[0:4, lanes] = coded_mom
        rest_mom = decay_rate * (m - decode_block(coded_mom, wide_pick, decode))
        rest_grad = g.astype(f32) * (1 / SHIFT) - decode_block(coded_grad, pick, decode) * SHIFT
        for layer in range(layers):
            rest_mom_ref[0, layer, :, lanes] = rest_mom[layer * rows : (layer + 1) * rows]
            rest_grad_ref[0, layer, :, lanes] = rest_grad[layer * rows : (layer + 1) * rows]


def spectra_kernel(count, squares_ref, coded_ref, copies_ref, clip_ref):
    here = lax.axis_index("core")
    clips = []
    members = squares_ref.shape[0] // 2
    for core in range(2):
        total = jnp.sum(squares_ref[core * members : (core + 1) * members], axis=0)
        squares = [jnp.sum(total[i : i + 1], keepdims=True) for i in range(2)]
        square = jnp.concatenate([jnp.broadcast_to(s, (4, LANES)) for s in squares], axis=0)
        clips.append(1.0 / jnp.maximum(1.0, jnp.sqrt(square / count + epsilon)))
    clip_ref[...] = jnp.where(here == 0, clips[0], clips[1])
    for b in range(coded_ref.shape[2] // LANES):
        lanes = slice(b * LANES, (b + 1) * LANES)
        both = [decay_rate * coded_ref[core, 0:4, lanes] + clips[core][2:6] * coded_ref[core, 4:8, lanes] for core in range(2)]
        pair = both[0] + both[1]
        part = jnp.where(here == 0, pair[0:2], pair[2:4])
        copies_ref[:, :, lanes] = jnp.broadcast_to(part[None], (copies_ref.shape[0], 2, LANES))


def decode_block(spectra, pick, decode):
    return times((spectra[:, None, :] * pick[None]).reshape(-1, LANES), decode, transposed=True)


def last_kernel(rest_mom_ref, rest_grad_ref, clip_ref, total_ref, pick_ref, decode_ref, new_hbm, update_hbm, new_ref, update_ref, sems):
    layers, rows, cols = update_ref.shape
    copies = []
    lane = lax.broadcasted_iota(jnp.int32, (4, LANES), 1)
    for b in range(cols // LANES):
        lanes = slice(b * LANES, (b + 1) * LANES)
        tiles = decode_block(total_ref[:, lanes], pick_ref[...], decode_ref[...]).reshape(4, GROUP, LANES)
        size = jnp.sum(jnp.abs(tiles), axis=1)
        left = jnp.sum(jnp.where(lane < GROUP, size, 0.0), axis=1, keepdims=True)
        right = jnp.sum(jnp.where(lane < GROUP, 0.0, size), axis=1, keepdims=True)
        mean = jnp.where(lane < GROUP, left, right) / (GROUP * GROUP)
        scale = 1.0 / (mean + epsilon)
        update_ref[:, :, lanes] = jnp.tanh(tiles * scale[:, None, :]).astype(bf16).reshape(layers, rows, LANES)
        for layer in range(layers):
            each = clip_ref[4 * layer : 4 * layer + 1, :]
            new_ref[0, layer, :, lanes] = rest_mom_ref[0, layer, :, lanes] + (each * rest_grad_ref[0, layer, :, lanes]) * SHIFT
        part = pl.ds(b * LANES, LANES)
        copies.append(pltpu.make_async_copy(new_ref.at[:, :, :, part], new_hbm.at[:, :, :, part], sems.at[len(copies)]))
        copies[-1].start()
        copies.append(pltpu.make_async_copy(update_ref.at[:, :, part], update_hbm.at[:, :, part], sems.at[len(copies)]))
        copies[-1].start()
    for copy in copies:
        copy.wait()


def exchange(x, axes, groups):
    return lax.all_to_all(x, axes, 0, 0, axis_index_groups=groups, tiled=True)


def solution(mesh):
    whole = Mesh(mesh.devices.reshape(8, 4, 2, 2, 4), ("z", "yh", "core", "yl", "x"))
    rep, mp = ("z", "yh", "core"), ("yl", "x")

    first_groups = [[core * 8 + yl * 4 + (x + 2) % 4 for core in range(2) for yl in range(2) for x in range(4)]]
    second_groups = [
        [(((z + 6) % 8) * 4 + (yh + 2) % 4) * 2 + core for z in range(8) for yh in range(4)] for core in range(2)
    ]

    def per_device(momentum, gradient, kept_index):
        _, layers, rows, cols = momentum.shape
        count = float(rows * cols * 8)
        sds = jax.ShapeDtypeStruct

        shapes = (momentum.shape, f32), (gradient.shape, bf16), ((GROUP, LANES), f32), ((2 * LANES, 2 * LANES), bf16), ((2 * LANES, 2 * LANES), bf16)
        hbm = lambda x: pltpu.with_memory_space_constraint(x, pltpu.HBM)
        squares, momentum, gradient, pick, code, decode = pl.pallas_call(
            first_kernel,
            in_specs=[pl.BlockSpec(memory_space=pltpu.HBM)] * 3,
            out_shape=(pltpu.HBM((16, 2, LANES), f32), *[pltpu.VMEM(*s) for s in shapes]),
            out_specs=(pl.BlockSpec(memory_space=pltpu.HBM),) + (pl.BlockSpec(memory_space=pltpu.VMEM),) * 5,
            scratch_shapes=[
                pltpu.VMEM((16, 2, LANES), f32),
                pltpu.VMEM((1, GROUP), jnp.int32),
                pltpu.SemaphoreType.DMA((layers + 3,)),
            ],
            compiler_params=pltpu.CompilerParams(vmem_limit_bytes=24 * 1024 * 1024),
            name="squares",
        )(hbm(momentum), hbm(gradient), hbm(kept_index.reshape(1, GROUP)))
        squares = exchange(squares, ("core",) + mp, first_groups)
        vmem = lambda *shapes: tuple(pltpu.VMEM(*s) for s in shapes)
        room = pltpu.CompilerParams(vmem_limit_bytes=24 * 1024 * 1024)
        coded, rest_mom, rest_grad = pl.pallas_call(
            code_kernel,
            out_shape=vmem(((8, cols), f32), (momentum.shape, f32), (momentum.shape, f32)),
            out_specs=(pl.BlockSpec(memory_space=pltpu.VMEM),) * 3,
            compiler_params=room,
            cost_estimate=pl.CostEstimate(flops=1 << 28, bytes_accessed=1 << 22, transcendentals=0),
            name="transforms",
        )(momentum, gradient, pick, code, decode)
        coded = lax.all_gather(coded, "core")
        copies, clip = pl.pallas_call(
            lambda *refs: spectra_kernel(count, *refs),
            out_shape=vmem(((32, 2, cols), f32), ((8, LANES), f32)),
            out_specs=(pl.BlockSpec(memory_space=pltpu.VMEM),) * 2,
            compiler_params=room,
            name="spectra",
        )(squares, coded)
        got = exchange(copies, rep, second_groups)
        total = lax.all_gather(jnp.sum(got, axis=0), "core", tiled=True)
        return pl.pallas_call(
            last_kernel,
            out_shape=(pltpu.HBM(momentum.shape, f32), pltpu.HBM((layers, rows, cols), bf16)),
            out_specs=(pl.BlockSpec(memory_space=pltpu.HBM),) * 2,
            scratch_shapes=[
                pltpu.VMEM(momentum.shape, f32),
                pltpu.VMEM((layers, rows, cols), bf16),
                pltpu.SemaphoreType.DMA((2 * (cols // LANES),)),
            ],
            compiler_params=room,
            name="new_momentum_and_update",
        )(rest_mom, rest_grad, clip, total, pick, decode)

    return jax.shard_map(
        per_device,
        mesh=whole,
        in_specs=(P(rep, None, None, mp), P(rep, None, None, mp), P()),
        out_specs=(P(rep, None, None, mp), P(None, None, mp)),
        check_vma=False,
    )
```
